256 devices in a mesh: gy: 16 (over z_lo, x), gx: 16 (over y, z_hi, core).
Axes of the slice: x: 4, y: 4, z: 8 (z_hi: 2, z_lo: 4; z = z_hi * 4 + z_lo), core: 2. Of those that a mesh axis runs over, the one named last changes fastest.
Arguments:
- tokens: bfloat16 [64, 128, 64, 256], P('gx', 'gy'), may hold values from -6 to 6
- norm_gains: float32 [3, 256], replicated, may hold values from 0.1 to 1.9
- qkv_weight: bfloat16 [3, 256, 768], replicated, may hold values from -2 to 2
- out_weight: bfloat16 [3, 256, 256], replicated, may hold values from -0.75 to 0.75
Outputs:
- swept: bfloat16 [64, 128, 64, 256], P('gx', 'gy')
The draws below stay inside these ranges and needn't reach their ends.
All inputs are finite; a program needn't handle non-finite values.
Results may differ from the reference program's by a relative error of at most 0.018.
Values may be sent and summed in bfloat16 or wider, within the bound.
No kernel may reach another device: no remote copies, remote signals or barrier semaphores. Data moves between devices by JAX's collectives and lax.ppermute only.
A program may use at most 64 MiB of HBM per device.

```python
import jax
import jax.numpy as jnp
from jax import lax

C = 256
HEADS = 8
NZ = 64
NX = 64
NY = 128


def draw_qkv_weight(key, part):
    key = jax.random.fold_in(key, 7)
    first, second, third = jax.random.split(key, 3)
    factor = C ** (-0.5)
    query_part = jnp.clip(jax.random.normal(first, (3, C, C), jnp.float32), -4.0, 4.0) * factor
    key_part = jnp.clip(jax.random.normal(second, (3, C, C), jnp.float32), -4.0, 4.0) * factor
    value_part = jnp.clip(jax.random.normal(third, (3, C, C), jnp.float32), -4.0, 4.0) * factor
    return jnp.clip(jnp.concatenate([query_part, key_part, value_part], axis=2), -2.0, 2.0).astype(jnp.bfloat16)


def block_scale(key, dims, shards, low, largest):
    def one(position, shards_of):
        steps = jax.random.uniform(jax.random.fold_in(jax.random.fold_in(key, 6), position), (shards_of,), jnp.float32, low / len(shards), largest / len(shards))
        return jnp.repeat(jnp.exp(steps), dims[position] // shards_of).reshape((-1,) + (1,) * (len(dims) - position - 1))

    factor_of = one(*shards[0])
    for cut in shards[1:]:
        factor_of = factor_of * one(*cut)
    return factor_of


def bell_draw(own_key, extent, deviation, reach, cuts=(), dtype=jnp.bfloat16):
    factor_of = block_scale(own_key, extent, cuts, -0.22, 0.18) if cuts else 1.0
    drawn = jax.random.normal(own_key, extent, jnp.float32) * deviation * factor_of
    return jnp.minimum(jnp.maximum(drawn, -reach), reach).astype(dtype)


def setup_inputs(seed: int = 0) -> dict:
    arg_keys = jax.random.split(jax.random.key(seed), 5)
    tokens = bell_draw(arg_keys[0], (NX, NY, NZ, C), 1.0, 6.0, ((0, 16), (1, 16)))
    norm_gains = jnp.clip(1.0 + 0.18 * jax.random.normal(arg_keys[1], (3, C), jnp.float32), 0.1, 1.9)
    qkv_weight = draw_qkv_weight(jax.random.fold_in(arg_keys[4], 71), 0)
    out_weight = bell_draw(arg_keys[3], (3, C, C), (C // 4) ** -0.5, 0.75)
    return {"tokens": tokens, "norm_gains": norm_gains, "qkv_weight": qkv_weight, "out_weight": out_weight}


def axial_pass(stream, norm_gain, qkv_weight, out_weight, line_axis):
    moved = jnp.moveaxis(stream, line_axis, -2)
    widened = moved.astype(jnp.float32)
    centre = lax.optimization_barrier(jnp.mean(widened, axis=-1, keepdims=True))
    centred = widened - centre
    spread = lax.optimization_barrier(jnp.mean(centred * centred, axis=-1, keepdims=True))
    normed = (centred * lax.rsqrt(spread + 1e-05) * norm_gain).astype(jnp.bfloat16)
    packed = jnp.dot(normed, qkv_weight, preferred_element_type=jnp.float32).astype(jnp.bfloat16)
    width = normed.shape[-1]
    head_size = width // HEADS
    packed = packed.reshape(packed.shape[:-1] + (3, HEADS, head_size))
    query_rows = packed[..., 0, :, :].astype(jnp.float32)
    key_rows = packed[..., 1, :, :].astype(jnp.float32)
    value_rows = packed[..., 2, :, :].astype(jnp.float32)
    scores = jnp.einsum('...qhd,...khd->...hqk', query_rows, key_rows) * head_size ** (-0.5)
    top = lax.optimization_barrier(jnp.max(scores, axis=-1, keepdims=True))
    expo = jnp.exp(scores - top)
    weights = (expo / lax.optimization_barrier(jnp.sum(expo, axis=-1, keepdims=True))).astype(jnp.bfloat16)
    mixed = jnp.einsum('...hqk,...khd->...qhd', weights.astype(jnp.float32), value_rows).astype(jnp.bfloat16)
    mixed = mixed.reshape(mixed.shape[:-2] + (width,))
    update = jnp.dot(mixed, out_weight, preferred_element_type=jnp.float32)
    result = (widened + update).astype(jnp.bfloat16)
    return jnp.moveaxis(result, -2, line_axis)

def reference(tokens, norm_gains, qkv_weight, out_weight):

    def run_pass(stream, index):
        return lax.map(lambda column_block: axial_pass(column_block, norm_gains[index], qkv_weight[index], out_weight[index], 1), stream)
    stream = run_pass(tokens, 0)
    stream = jnp.transpose(run_pass(jnp.transpose(stream, (0, 2, 1, 3)), 1), (0, 2, 1, 3))
    stream = jnp.transpose(run_pass(jnp.transpose(stream, (1, 2, 0, 3)), 2), (2, 0, 1, 3))
    return stream
```

```python
import functools

import jax
import jax.numpy as jnp
from jax import lax
from jax.experimental import pallas as pl
from jax.experimental.pallas import tpu as pltpu
from jax.sharding import Mesh, PartitionSpec as P

HEADS = 8
C = 256
HEAD = 32
UNIT = 128
BLOCK = 256
BF16 = jnp.bfloat16
F32 = jnp.float32
SCALE = HEAD ** (-0.5) * 1.4426950408889634
NT = (((1,), (1,)), ((), ()))


def mm(a, b):
    return jnp.dot(a, b, preferred_element_type=F32)


def mm_nt(a, b):
    return lax.dot_general(a, b, NT, preferred_element_type=F32)


def attend_unit(q, k, vt, line):
    lines = UNIT // line
    lane = lax.broadcasted_iota(jnp.int32, (1, C), 1)
    zero = jnp.zeros((), BF16)
    if lines == 2:
        k = jnp.concatenate([k[:line], k[line:]], axis=1)
        q_lane = lax.broadcasted_iota(jnp.int32, (1, 2 * UNIT), 1) % UNIT
    rows = []
    for pair in range(HEADS // 2):
        parts = []
        for head in (2 * pair, 2 * pair + 1):
            own = (lane >= head * HEAD) & (lane < (head + 1) * HEAD)
            part = jnp.where(own, q, zero)
            if lines == 2:
                empty = jnp.zeros((line, C), BF16)
                part = jnp.concatenate(
                    [
                        jnp.concatenate([part[:line], empty], axis=1),
                        jnp.concatenate([empty, part[line:]], axis=1),
                    ],
                    axis=0,
                )
            parts.append(part)
        scores = mm_nt(k, jnp.concatenate(parts, axis=0))
        top = jnp.max(scores, axis=0, keepdims=True)
        expo = jnp.exp2((scores - top) * SCALE)
        total = jnp.sum(expo, axis=0, keepdims=True)
        expo = expo.astype(BF16)
        if lines == 2:
            expo = jnp.concatenate(
                [jnp.where(q_lane < line, expo, zero), jnp.where(q_lane < line, zero, expo)], axis=0
            )
        own_v = vt[pair * 2 * HEAD : (pair + 1) * 2 * HEAD]
        both = mm(own_v, expo) * (1.0 / total)
        rows.append(both[:HEAD, :UNIT].astype(BF16))
        rows.append(both[HEAD:, UNIT:].astype(BF16))
    return jnp.concatenate(rows, axis=0)


def pass_block(s, gain, wqk, wvt, wo, line):
    centred = s - jnp.mean(s, axis=1, keepdims=True)
    spread = jnp.mean(centred * centred, axis=1, keepdims=True)
    normed = (centred * lax.rsqrt(spread + 1e-05) * gain).astype(BF16)
    qk = mm(normed, wqk).astype(BF16)
    vt = mm_nt(wvt, normed).astype(BF16)
    mixed = []
    for u in range(BLOCK // UNIT):
        at = slice(u * UNIT, (u + 1) * UNIT)
        mixed.append(attend_unit(qk[at, :C], qk[at, C:], vt[:, at], line).T)
    return s + mm(jnp.concatenate(mixed, axis=0), wo)


def plain_kernel(line, x_ref, gain_ref, wqkv_ref, wo_ref, o_ref, wvt_ref):
    wvt_ref[...] = wqkv_ref[:, 2 * C :].T

    @pl.loop(0, x_ref.shape[0])
    def _(i):
        s = x_ref[i].astype(F32)
        out = pass_block(s, gain_ref[...], wqkv_ref[:, : 2 * C], wvt_ref[...], wo_ref[...], line)
        o_ref[i] = out.astype(BF16)


def axial_pass(tokens, gain, wqkv, wo, line):
    n = tokens.shape[0]
    whole = pl.BlockSpec(memory_space=pltpu.VMEM)
    return pl.pallas_call(
        functools.partial(plain_kernel, line),
        out_shape=jax.ShapeDtypeStruct((n, BLOCK, C), BF16),
        in_specs=[whole] * 4,
        out_specs=whole,
        scratch_shapes=[pltpu.VMEM((C, C), BF16)],
        compiler_params=pltpu.CompilerParams(vmem_limit_bytes=24 << 20),
        cost_estimate=pl.CostEstimate(flops=n * 256 * 1048576 * 2, bytes_accessed=n * 262144, transcendentals=n * 262144),
    )(tokens, gain, wqkv, wo)


def body(tokens, norm_gains, qkv_weight, out_weight):
    def run(x, p, line):
        return axial_pass(x.reshape(-1, BLOCK, C), norm_gains[p : p + 1], qkv_weight[p], out_weight[p], line)

    s = run(tokens, 0, 64)
    s = s.reshape(4, 8, 32, 2, C).transpose(2, 0, 3, 1, 4).reshape(32, 64, C)
    s = lax.all_to_all(s, ("zl", "x", "zh"), 0, 0, tiled=True)
    s = s.reshape(16, 2, 4, 2, 8, C).transpose(1, 2, 3, 0, 4, 5)
    s = run(s, 1, 128)
    s = s.reshape(2, 4, 2, 16, 8, C).transpose(4, 0, 1, 2, 3, 5).reshape(8, 256, C)
    s = lax.all_to_all(s, ("core", "y"), 0, 0, tiled=True)
    s = s.reshape(2, 4, 2, 4, 2, 16, C).transpose(4, 5, 1, 2, 0, 3, 6)
    s = run(s, 2, 64)
    s = s.reshape(2, 4, 4, 4, 2, 2, 4, C).transpose(5, 3, 1, 2, 4, 6, 0, 7).reshape(256, 8, C)
    s = lax.all_to_all(s, ("core", "y", "zl", "x", "zh"), 0, 0, tiled=True)
    return s.reshape(8, 32, 4, 2, C).transpose(2, 0, 1, 3, 4).reshape(4, 8, 64, C)


def solution(mesh):
    fine = Mesh(mesh.devices.reshape(4, 4, 4, 2, 2), ("zl", "x", "y", "zh", "core"))
    spec = P(("y", "zh", "core"), ("zl", "x"), None, None)
    return jax.shard_map(
        body, mesh=fine, in_specs=(spec, P(), P(), P()), out_specs=spec, check_vma=False
    )
```

```python
import functools

import jax
import jax.numpy as jnp
from jax import lax
from jax.experimental import pallas as pl
from jax.experimental.pallas import tpu as pltpu
from jax.sharding import Mesh, PartitionSpec as P

HEADS = 8
C = 256
HEAD = 32
UNIT = 128
BLOCK = 256
TOKENS = 2048
BF16 = jnp.bfloat16
F32 = jnp.float32
SCALE = HEAD ** (-0.5) * 1.4426950408889634
LOW = -1e30
NT = (((1,), (1,)), ((), ()))


def mm(a, b):
    return jnp.dot(a, b, preferred_element_type=F32)


def mm_nt(a, b):
    return lax.dot_general(a, b, NT, preferred_element_type=F32)


def lanes(n=C):
    return lax.broadcasted_iota(jnp.int32, (1, n), 1)


def two_halves(a):
    empty = jnp.zeros((a.shape[0], 128), BF16)
    return jnp.concatenate(
        [jnp.concatenate([a[:, :128], empty], axis=1), jnp.concatenate([empty, a[:, 128:]], axis=1)], axis=0
    )


def four_quarters(a):
    lane = lanes()
    zero = jnp.zeros((), BF16)
    return jnp.concatenate([jnp.where(lane // 64 == i, a, zero) for i in range(4)], axis=0)


def attend_64(q, k, v):
    lane = lanes()
    zero = jnp.zeros((), BF16)
    first = lane % 64 < HEAD
    own_q = jnp.concatenate([jnp.where(first, q, zero), jnp.where(first, zero, q)], axis=0)
    scores = mm_nt(own_q, four_quarters(k))
    left = lanes(128) < 64
    expo = []
    for half in range(2):
        s = scores[:, half * 128 : (half + 1) * 128]
        top_left = jnp.max(jnp.where(left, s, LOW), axis=1, keepdims=True)
        top_right = jnp.max(jnp.where(left, LOW, s), axis=1, keepdims=True)
        expo.append(jnp.exp2(s - jnp.where(left, top_left, top_right)).astype(BF16))
    expo = jnp.concatenate(expo, axis=1)
    mixed = mm(expo, four_quarters(v))
    total = mm(expo, four_quarters(jnp.ones((64, C), BF16)))
    return jnp.where(first, mixed[:64], mixed[64:]) / jnp.where(first, total[:64], total[64:])


def attend_128(q, k, v):
    slot = lanes() % 128 // HEAD
    zero = jnp.zeros((), BF16)
    one = jnp.ones((), BF16)
    own_q = jnp.concatenate([jnp.where(slot == j, q, zero) for j in range(4)], axis=0)
    scores = mm_nt(own_q, two_halves(k))
    expo = []
    for half in range(2):
        s = scores[:, half * 128 : (half + 1) * 128]
        expo.append(jnp.exp2(s - jnp.max(s, axis=1, keepdims=True)).astype(BF16))
    expo = jnp.concatenate(expo, axis=1)
    a = mm(expo[: 2 * UNIT], two_halves(jnp.where(slot < 2, v, one)))
    b = mm(expo[2 * UNIT :], two_halves(jnp.where(slot < 2, one, v)))
    parts = [a[:UNIT], a[UNIT:], b[:UNIT], b[UNIT:]]

    def pick(w, x, y, z):
        return jnp.where(slot == 0, w, jnp.where(slot == 1, x, jnp.where(slot == 2, y, z)))

    total = pick(parts[2], parts[3], parts[0], parts[1])
    total = jnp.concatenate([pltpu.roll(total[:, :128], 64, 1), pltpu.roll(total[:, 128:], 64, 1)], axis=1)
    return pick(*parts) / total


def project(s, gain, wqkv_ref, q_ref, k_ref, v_ref, rows):
    centred = s - jnp.mean(s, axis=1, keepdims=True)
    spread = jnp.mean(centred * centred, axis=1, keepdims=True)
    normed = (centred * lax.rsqrt(spread + 1e-05) * gain).astype(BF16)
    packed = mm(normed, wqkv_ref[...])
    q_ref[rows] = packed[:, :C].astype(BF16)
    k_ref[rows] = (packed[:, C : 2 * C] * SCALE).astype(BF16)
    v_ref[rows] = packed[:, 2 * C :].astype(BF16)


def attend(q_ref, k_ref, v_ref, line):
    one, count = (attend_64, 16) if line == 64 else (attend_128, 4)

    @pl.loop(0, TOKENS // (line * count))
    def _(i):
        for j in range(count):
            rows = pl.ds(pl.multiple_of((i * count + j) * line, line), line)
            q_ref[rows] = one(q_ref[rows], k_ref[rows], v_ref[rows]).astype(BF16)


def reorder(source):
    r = lax.broadcasted_iota(jnp.int32, (BLOCK, BLOCK), 0)
    c = lax.broadcasted_iota(jnp.int32, (BLOCK, BLOCK), 1)
    return (c == source(r)).astype(F32).astype(BF16)


def chunk(i, size):
    return pl.ds(pl.multiple_of(i * size, size), size)


def z_kernel(x_ref, gain_ref, wqkv_ref, wo_ref, o_ref, q_ref, k_ref, v_ref, turn_ref):
    turn_ref[...] = reorder(lambda r: r % 8 * 32 + r // 8)

    @pl.loop(0, 2)
    def _(i):
        rows = chunk(i, 1024)
        project(x_ref[rows].astype(F32), gain_ref[0:1], wqkv_ref, q_ref, k_ref, v_ref, rows)

    attend(q_ref, k_ref, v_ref, 64)

    @pl.loop(0, 4)
    def _(i):
        rows = chunk(i, 512)
        out = (x_ref[rows].astype(F32) + mm(q_ref[rows], wo_ref[...])).astype(BF16)
        for half in range(2):
            block = jnp.concatenate([out[y * 64 + half * 32 : y * 64 + half * 32 + 32] for y in range(8)], axis=0)
            turned = mm(turn_ref[...], block).astype(BF16)
            o_ref[half * 16 : half * 16 + 16, i] = turned.reshape(16, 16, C)


def y_kernel(x_ref, gain_ref, wqkv_ref, wo_ref, o_ref, q_ref, k_ref, v_ref, turn_ref):
    turn_ref[...] = reorder(lambda r: r % 32 * 8 + r // 32)

    def lines(zh, xl):
        s = x_ref[:, zh, xl].reshape(BLOCK, C).astype(F32)
        return jnp.concatenate([s[yb * 16 + zl * 8 : yb * 16 + zl * 8 + 8] for zl in range(2) for yb in range(16)], axis=0)

    @pl.loop(0, 2)
    def _(zh):
        s = jnp.concatenate([lines(zh, xl) for xl in range(4)], axis=0)
        project(s, gain_ref[1:2], wqkv_ref, q_ref, k_ref, v_ref, chunk(zh, 1024))

    attend(q_ref, k_ref, v_ref, 128)

    @pl.loop(0, 2)
    def _(zh):
        update = mm(q_ref[chunk(zh, 1024)], wo_ref[...])
        for xl in range(4):
            out = (lines(zh, xl) + update[xl * BLOCK : (xl + 1) * BLOCK]).astype(BF16)
            o_ref[:, zh, xl] = mm(turn_ref[...], out).astype(BF16).reshape(8, 32, C)


def x_kernel(x_ref, gain_ref, wqkv_ref, wo_ref, o_ref, q_ref, k_ref, v_ref, turn_ref, s_ref):
    turn_ref[...] = reorder(lambda r: r % 16 * 16 + r // 16)

    @pl.loop(0, 2)
    def _(zl):
        some = chunk(zl, 16)
        for a in range(4):
            block = x_ref[a * 16 : a * 16 + 16, some].reshape(BLOCK, C)
            s_ref[some, a * 16 : a * 16 + 16] = mm(turn_ref[...], block).astype(BF16).reshape(16, 16, C)
        rows = chunk(zl, 1024)
        project(s_ref[some].reshape(1024, C).astype(F32), gain_ref[2:3], wqkv_ref, q_ref, k_ref, v_ref, rows)

    attend(q_ref, k_ref, v_ref, 64)

    turn_ref[...] = reorder(lambda r: (r % 2 * 2 + r // 16 % 2) * 64 + r // 32 * 8 + r // 2 % 8)

    @pl.loop(0, 2)
    def _(i):
        parts = []
        for zl in range(2):
            rows = pl.ds(pl.multiple_of(zl * 1024 + i * 512, 512), 512)
            s = s_ref[pl.ds(pl.multiple_of(zl * 16 + i * 8, 8), 8)].reshape(512, C)
            parts.append((s.astype(F32) + mm(q_ref[rows], wo_ref[...])).astype(BF16))
        for j in range(4):
            at = slice(j * 128, (j + 1) * 128)
            block = jnp.concatenate([parts[0][at], parts[1][at]], axis=0)
            turned = mm(turn_ref[...], block).astype(BF16).reshape(8, 2, 16, C)
            o_ref[:, pl.ds(i * 8 + j * 2, 2)] = turned


def home_kernel(x_ref, o_ref):
    turn = reorder(lambda r: r % 64 // 2 * 8 + r // 64 * 2 + r % 2)
    for y in range(x_ref.shape[0]):
        o_ref[:, y] = mm(turn, x_ref[y]).astype(BF16).reshape(4, 64, C)


def axial_pass(kernel, p, x, gains, wqkv, wo, shape):
    whole = pl.BlockSpec(memory_space=pltpu.VMEM)
    tokens = pltpu.VMEM((TOKENS, C), BF16)
    return pl.pallas_call(
        kernel,
        grid=(1,),
        out_shape=jax.ShapeDtypeStruct(shape, BF16),
        in_specs=[
            whole,
            whole,
            pl.BlockSpec((None, C, 3 * C), lambda i: (p, 0, 0)),
            pl.BlockSpec((None, C, C), lambda i: (p, 0, 0)),
        ],
        out_specs=whole,
        scratch_shapes=[tokens] * 3 + [pltpu.VMEM((BLOCK, BLOCK), BF16)] + [pltpu.VMEM((32, 64, C), BF16)] * (kernel is x_kernel),
        compiler_params=pltpu.CompilerParams(vmem_limit_bytes=32 << 20),
    )(x, gains, wqkv, wo)


def home(x):
    return pl.pallas_call(
        home_kernel,
        grid=(2,),
        out_shape=jax.ShapeDtypeStruct((4, 8, 64, C), BF16),
        in_specs=[pl.BlockSpec((4, BLOCK, C), lambda i: (i, 0, 0))],
        out_specs=pl.BlockSpec((4, 4, 64, C), lambda i: (0, i, 0, 0)),
        compiler_params=pltpu.CompilerParams(vmem_limit_bytes=16 << 20),
    )(x)


def body(tokens, gains, wqkv, wo):
    s = axial_pass(z_kernel, 0, tokens.reshape(TOKENS, C), gains, wqkv, wo, (32, 4, 16, C))
    s = lax.all_to_all(s.reshape(32, 64, C), ("zl", "x", "zh"), 0, 0, tiled=True)
    s = axial_pass(y_kernel, 1, s.reshape(16, 2, 4, 16, C), gains, wqkv, wo, (8, 2, 4, 32, C))
    s = lax.all_to_all(s.reshape(8, 256, C), ("core", "y"), 0, 0, tiled=True)
    s = axial_pass(x_kernel, 2, s.reshape(64, 32, C), gains, wqkv, wo, (8, 16, 16, C))
    s = lax.all_to_all(s.reshape(256, 8, C), ("core", "y", "zl", "x", "zh"), 0, 0, tiled=True)
    return home(s.reshape(8, BLOCK, C))


def solution(mesh):
    fine = Mesh(mesh.devices.reshape(4, 4, 4, 2, 2), ("zl", "x", "y", "zh", "core"))
    spec = P(("y", "zh", "core"), ("zl", "x"), None, None)
    return jax.shard_map(
        body, mesh=fine, in_specs=(spec, P(), P(), P()), out_specs=spec, check_vma=False
    )
```

```python
import functools

import jax
import jax.numpy as jnp
from jax import lax
from jax.experimental import pallas as pl
from jax.experimental.pallas import tpu as pltpu
from jax.sharding import Mesh, PartitionSpec as P

HEADS = 8
C = 256
HEAD = 32
UNIT = 128
BLOCK = 256
TOKENS = 2048
BF16 = jnp.bfloat16
F32 = jnp.float32
SCALE = HEAD ** (-0.5) * 1.4426950408889634
LOW = -1e30
NT = (((1,), (1,)), ((), ()))


def mm(a, b):
    return jnp.dot(a, b, preferred_element_type=F32)


def mm_nt(a, b):
    return lax.dot_general(a, b, NT, preferred_element_type=F32)


def lanes(n=C):
    return lax.broadcasted_iota(jnp.int32, (1, n), 1)


def two_halves(a):
    empty = jnp.zeros((a.shape[0], 128), BF16)
    return jnp.concatenate(
        [jnp.concatenate([a[:, :128], empty], axis=1), jnp.concatenate([empty, a[:, 128:]], axis=1)], axis=0
    )


def four_quarters(a):
    lane = lanes()
    zero = jnp.zeros((), BF16)
    return jnp.concatenate([jnp.where(lane // 64 == i, a, zero) for i in range(4)], axis=0)


def attend_64(q, k, v):
    lane = lanes()
    zero = jnp.zeros((), BF16)
    first = lane % 64 < HEAD
    own_q = jnp.concatenate([jnp.where(first, q, zero), jnp.where(first, zero, q)], axis=0)
    scores = mm_nt(own_q, four_quarters(k))
    left = lanes(128) < 64
    expo = []
    for half in range(2):
        s = scores[:, half * 128 : (half + 1) * 128]
        top_left = jnp.max(jnp.where(left, s, LOW), axis=1, keepdims=True)
        top_right = jnp.max(jnp.where(left, LOW, s), axis=1, keepdims=True)
        expo.append(jnp.exp2(s - jnp.where(left, top_left, top_right)).astype(BF16))
    expo = jnp.concatenate(expo, axis=1)
    mixed = mm(expo, four_quarters(v))
    total = mm(expo, four_quarters(jnp.ones((64, C), BF16)))
    return jnp.where(first, mixed[:64], mixed[64:]) / jnp.where(first, total[:64], total[64:])


def attend_128(q, k, v):
    slot = lanes() % 128 // HEAD
    zero = jnp.zeros((), BF16)
    one = jnp.ones((), BF16)
    own_q = jnp.concatenate([jnp.where(slot == j, q, zero) for j in range(4)], axis=0)
    scores = mm_nt(own_q, two_halves(k))
    expo = []
    for half in range(2):
        s = scores[:, half * 128 : (half + 1) * 128]
        expo.append(jnp.exp2(s - jnp.max(s, axis=1, keepdims=True)).astype(BF16))
    expo = jnp.concatenate(expo, axis=1)
    a = mm(expo[: 2 * UNIT], two_halves(jnp.where(slot < 2, v, one)))
    b = mm(expo[2 * UNIT :], two_halves(jnp.where(slot < 2, one, v)))
    parts = [a[:UNIT], a[UNIT:], b[:UNIT], b[UNIT:]]

    def pick(w, x, y, z):
        return jnp.where(slot == 0, w, jnp.where(slot == 1, x, jnp.where(slot == 2, y, z)))

    total = pick(parts[2], parts[3], parts[0], parts[1])
    total = jnp.concatenate([pltpu.roll(total[:, :128], 64, 1), pltpu.roll(total[:, 128:], 64, 1)], axis=1)
    return pick(*parts) / total


def project(s, gain, wqkv_ref, q_ref, k_ref, v_ref, rows):
    centred = s - jnp.mean(s, axis=1, keepdims=True)
    spread = jnp.mean(centred * centred, axis=1, keepdims=True)
    normed = (centred * lax.rsqrt(spread + 1e-05) * gain).astype(BF16)
    packed = mm(normed, wqkv_ref[...])
    q_ref[rows] = packed[:, :C].astype(BF16)
    k_ref[rows] = (packed[:, C : 2 * C] * SCALE).astype(BF16)
    v_ref[rows] = packed[:, 2 * C :].astype(BF16)


def attend(q_ref, k_ref, v_ref, m_ref, line):
    one, count = (attend_64, 16) if line == 64 else (attend_128, 4)

    @pl.loop(0, TOKENS // (line * count))
    def _(i):
        for j in range(count):
            rows = pl.ds(pl.multiple_of((i * count + j) * line, line), line)
            m_ref[rows] = one(q_ref[rows], k_ref[rows], v_ref[rows]).astype(BF16)


def reorder(source):
    r = lax.broadcasted_iota(jnp.int32, (BLOCK, BLOCK), 0)
    c = lax.broadcasted_iota(jnp.int32, (BLOCK, BLOCK), 1)
    return (c == source(r)).astype(F32).astype(BF16)


def chunk(i, size):
    return pl.ds(pl.multiple_of(i * size, size), size)


def z_kernel(x_hbm, gain_hbm, wqkv_hbm, wo_hbm, o_ref, q_ref, k_ref, v_ref, m_ref, turn_ref, x_ref, gain_ref, wqkv_ref, wo_ref, sem):
    fetch = [
        pltpu.make_async_copy(gain_hbm, gain_ref, sem.at[0]),
        pltpu.make_async_copy(x_hbm.at[pl.ds(0, 1024)], x_ref.at[pl.ds(0, 1024)], sem.at[1]),
        pltpu.make_async_copy(wqkv_hbm.at[0], wqkv_ref, sem.at[2]),
        pltpu.make_async_copy(x_hbm.at[pl.ds(1024, 1024)], x_ref.at[pl.ds(1024, 1024)], sem.at[3]),
        pltpu.make_async_copy(wo_hbm.at[0], wo_ref, sem.at[4]),
    ]
    for copy in fetch:
        copy.start()
    turn_ref[...] = reorder(lambda r: r % 8 * 32 + r // 8)
    for i in range(2):
        for copy in (fetch[:3], fetch[3:])[i]:
            copy.wait()
        rows = slice(i * 1024, (i + 1) * 1024)
        project(x_ref[rows].astype(F32), gain_ref[0:1], wqkv_ref, q_ref, k_ref, v_ref, rows)

    attend(q_ref, k_ref, v_ref, m_ref, 64)

    @pl.loop(0, 4)
    def _(i):
        rows = chunk(i, 512)
        out = (x_ref[rows].astype(F32) + mm(m_ref[rows], wo_ref[...])).astype(BF16)
        for half in range(2):
            block = jnp.concatenate([out[y * 64 + half * 32 : y * 64 + half * 32 + 32] for y in range(8)], axis=0)
            turned = mm(turn_ref[...], block).astype(BF16)
            o_ref[half * 16 : half * 16 + 16, i] = turned.reshape(16, 16, C)


def y_kernel(x_ref, gain_ref, wqkv_ref, wo_ref, keep_ref, send_ref, q_ref, k_ref, v_ref, m_ref, turn_ref):
    me = lax.axis_index("core")

    def source(r):
        y_l = (r // 128 + me) % 2 * 4 + r // 8 % 4
        return r % 2 * 128 + r // 2 % 4 * 32 + r // 32 % 4 * 8 + y_l

    turn_ref[...] = reorder(source)

    def lines(zh, xl):
        s = x_ref[:, zh, xl].reshape(BLOCK, C).astype(F32)
        return jnp.concatenate([s[yb * 16 + zl * 8 : yb * 16 + zl * 8 + 8] for zl in range(2) for yb in range(16)], axis=0)

    @pl.loop(0, 2)
    def _(zh):
        s = jnp.concatenate([lines(zh, xl) for xl in range(4)], axis=0)
        project(s, gain_ref[1:2], wqkv_ref.at[1], q_ref, k_ref, v_ref, chunk(zh, 1024))

    attend(q_ref, k_ref, v_ref, m_ref, 128)

    @pl.loop(0, 2)
    def _(zh):
        update = mm(m_ref[chunk(zh, 1024)], wo_ref[1])
        for pair in range(2):
            turned = []
            for xl in (2 * pair, 2 * pair + 1):
                out = (lines(zh, xl) + update[xl * BLOCK : (xl + 1) * BLOCK]).astype(BF16)
                turned.append(mm(turn_ref[...], out))
            both = jnp.concatenate([t[g * 8 : g * 8 + 8] for g in range(32) for t in turned], axis=0).astype(BF16)
            keep_ref[:, :, 0, zh, pair] = both[:BLOCK].reshape(4, 4, 16, C)
            send_ref[:, :, zh, pair] = both[BLOCK:].reshape(4, 4, 16, C)


def x_kernel(x_ref, gain_ref, wqkv_ref, wo_ref, keep_ref, send_ref, q_ref, k_ref, v_ref, m_ref, turn_ref, s_ref):
    turn_ref[...] = reorder(lambda r: r % 32 // 2 * 16 + r % 2 * 8 + r // 32)

    @pl.loop(0, 2)
    def _(i):
        for j in range(2):
            for half in range(2):
                block = x_ref[i * 2 + j, half * 16 : half * 16 + 16].reshape(BLOCK, C)
                at = pl.ds(pl.multiple_of((i * 2 + j) * 8, 8), 8)
                s_ref[at, half * 32 : half * 32 + 32] = mm(turn_ref[...], block).astype(BF16).reshape(8, 32, C)
        s = s_ref[chunk(i, 16)].reshape(1024, C).astype(F32)
        project(s, gain_ref[2:3], wqkv_ref.at[2], q_ref, k_ref, v_ref, chunk(i, 1024))

    attend(q_ref, k_ref, v_ref, m_ref, 64)

    def source(r):
        return r // 8 % 2 * 128 + r % 2 * 64 + r // 32 % 4 * 16 + r // 128 * 8 + r // 16 % 2 * 4 + r // 2 % 4

    turn_ref[...] = reorder(source)

    @pl.loop(0, 2)
    def _(pair):
        s = s_ref[chunk(pair, 16)].reshape(1024, C).astype(F32)
        out = (s + mm(m_ref[chunk(pair, 1024)], wo_ref[2])).astype(BF16)
        for y_zl in range(4):
            block = jnp.concatenate([out[z * 512 + y_zl * 128 : z * 512 + y_zl * 128 + 128] for z in range(2)], axis=0)
            turned = mm(turn_ref[...], block).astype(BF16).reshape(2, 4, 2, 16, C)
            keep_ref[y_zl, :, :, 0, pair] = turned[0]
            send_ref[y_zl, :, :, pair] = turned[1]


def home_kernel(x_ref, o_ref):
    me = lax.axis_index("core")
    turn = reorder(lambda r: r // 16 % 4 * 64 + r // 2 % 2 * 32 + r // 4 % 4 * 8 + r // 64 * 2 + r % 2)
    for other in range(2):
        for y in range(4):
            block = x_ref[:, y, :, other].reshape(BLOCK, C)
            o_ref[:, (me + other) % 2 * 4 + y] = mm(turn, block).astype(BF16).reshape(4, 64, C)


WHOLE = pl.BlockSpec(memory_space=pltpu.VMEM)
HBM = pl.BlockSpec(memory_space=pltpu.HBM)


def axial_pass(kernel, x, gains, wqkv, wo, shapes, place=WHOLE, scratch=()):
    tokens = pltpu.VMEM((TOKENS, C), BF16)
    return pl.pallas_call(
        kernel,
        out_shape=[jax.ShapeDtypeStruct(shape, BF16) for shape in shapes],
        in_specs=[place] * 4,
        out_specs=[WHOLE] * len(shapes),
        scratch_shapes=[tokens] * 4 + [pltpu.VMEM((BLOCK, BLOCK), BF16), *scratch],
        compiler_params=pltpu.CompilerParams(vmem_limit_bytes=32 << 20),
    )(x, gains, wqkv, wo)


def z_pass(x, gains, wqkv, wo):
    fetched = [((TOKENS, C), BF16), ((3, C), F32), ((C, 3 * C), BF16), ((C, C), BF16)]
    scratch = [pltpu.VMEM(*f) for f in fetched] + [pltpu.SemaphoreType.DMA((5,))]
    fetch = [pltpu.with_memory_space_constraint(a, pltpu.HBM) for a in (x, gains, wqkv, wo)]
    return axial_pass(z_kernel, *fetch, [(32, 4, 16, C)], HBM, scratch)[0]


def y_pass(x, gains, wqkv, wo):
    return axial_pass(y_kernel, x, gains, wqkv, wo, [(4, 4, 2, 2, 2, 16, C), (4, 4, 2, 2, 16, C)])


def x_pass(x, gains, wqkv, wo):
    shapes = [(4, 4, 2, 2, 2, 16, C), (4, 4, 2, 2, 16, C)]
    return axial_pass(x_kernel, x, gains, wqkv, wo, shapes, scratch=[pltpu.VMEM((32, 64, C), BF16)])


def home(x):
    return pl.pallas_call(
        home_kernel,
        out_shape=jax.ShapeDtypeStruct((4, 8, 64, C), BF16),
        in_specs=[WHOLE],
        out_specs=WHOLE,
        compiler_params=pltpu.CompilerParams(vmem_limit_bytes=16 << 20),
    )(x)


def swap(keep, send, dests):
    got = lax.ppermute(send, "core", [(0, 1), (1, 0)])
    keep = keep.reshape(dests, 2, -1, C).at[:, 1].set(got.reshape(dests, -1, C))
    return keep.reshape(dests, -1, C)


def body(tokens, gains, wqkv, wo):
    weights = gains, wqkv, wo
    s = z_pass(tokens.reshape(TOKENS, C), *weights)
    s = lax.all_to_all(s.reshape(32, 64, C), ("zl", "x", "zh"), 0, 0, tiled=True)
    keep, send = y_pass(s.reshape(16, 2, 4, 16, C), *weights)
    s = lax.all_to_all(swap(keep, send, 16), ("x", "y"), 0, 0, tiled=True)
    keep, send = x_pass(s.reshape(4, 32, 16, C), *weights)
    s = lax.all_to_all(swap(keep, send, 32), ("zl", "y", "zh"), 0, 0, tiled=True)
    return home(s.reshape(4, 4, 2, 2, 32, C))


def solution(mesh):
    fine = Mesh(mesh.devices.reshape(4, 4, 4, 2, 2), ("zl", "x", "y", "zh", "core"))
    spec = P(("y", "zh", "core"), ("zl", "x"), None, None)
    return jax.shard_map(
        body, mesh=fine, in_specs=(spec, P(), P(), P()), out_specs=spec, check_vma=False
    )
```

```python
import functools

import jax
import jax.numpy as jnp
from jax import lax
from jax.experimental import pallas as pl
from jax.experimental.pallas import tpu as pltpu
from jax.sharding import Mesh, PartitionSpec as P

HEADS = 8
C = 256
HEAD = 32
UNIT = 128
BLOCK = 256
TOKENS = 2048
BF16 = jnp.bfloat16
F32 = jnp.float32
SCALE = HEAD ** (-0.5) * 1.4426950408889634
LOW = -1e30
NT = (((1,), (1,)), ((), ()))


def mm(a, b):
    return jnp.dot(a, b, preferred_element_type=F32)


def mm_nt(a, b):
    return lax.dot_general(a, b, NT, preferred_element_type=F32)


def lanes(n=C):
    return lax.broadcasted_iota(jnp.int32, (1, n), 1)


def two_halves(a):
    empty = jnp.zeros((a.shape[0], 128), BF16)
    return jnp.concatenate(
        [jnp.concatenate([a[:, :128], empty], axis=1), jnp.concatenate([empty, a[:, 128:]], axis=1)], axis=0
    )


def four_quarters(a):
    lane = lanes()
    zero = jnp.zeros((), BF16)
    return jnp.concatenate([jnp.where(lane // 64 == i, a, zero) for i in range(4)], axis=0)


def attend_64(q, k, v):
    lane = lanes()
    zero = jnp.zeros((), BF16)
    first = lane % 64 < HEAD
    own_q = jnp.concatenate([jnp.where(first, q, zero), jnp.where(first, zero, q)], axis=0)
    scores = mm_nt(own_q, four_quarters(k))
    left = lanes(128) < 64
    expo = []
    for half in range(2):
        s = scores[:, half * 128 : (half + 1) * 128]
        top_left = jnp.max(jnp.where(left, s, LOW), axis=1, keepdims=True)
        top_right = jnp.max(jnp.where(left, LOW, s), axis=1, keepdims=True)
        expo.append(jnp.exp2(s - jnp.where(left, top_left, top_right)).astype(BF16))
    expo = jnp.concatenate(expo, axis=1)
    mixed = mm(expo, four_quarters(v))
    total = mm(expo, four_quarters(jnp.ones((64, C), BF16)))
    return jnp.where(first, mixed[:64], mixed[64:]) / jnp.where(first, total[:64], total[64:])


def attend_128(lines):
    slot = lanes() % 128 // HEAD
    zero = jnp.zeros((), BF16)
    expos = []
    for q, k, _ in lines:
        own_q = jnp.concatenate([jnp.where(slot == j, q, zero) for j in range(4)], axis=0)
        scores = mm_nt(own_q, two_halves(k))
        expo = []
        for half in range(2):
            s = scores[:, half * 128 : (half + 1) * 128]
            expo.append(jnp.exp2(s - jnp.max(s, axis=1, keepdims=True)).astype(BF16))
        expos.append(jnp.concatenate(expo, axis=1))

    def pick(a):
        a = [a[j * UNIT : (j + 1) * UNIT] for j in range(4)]
        return jnp.where(slot == 0, a[0], jnp.where(slot == 1, a[1], jnp.where(slot == 2, a[2], a[3])))

    totals = mm(jnp.concatenate(expos, axis=0), two_halves(jnp.ones((UNIT, C), BF16)))
    return [
        pick(mm(expo, two_halves(v))) / pick(totals[i * 4 * UNIT : (i + 1) * 4 * UNIT])
        for i, (expo, (_, _, v)) in enumerate(zip(expos, lines))
    ]


def project(s, gain, wqkv_ref, q_ref, k_ref, v_ref, rows):
    centred = s - jnp.mean(s, axis=1, keepdims=True)
    spread = jnp.mean(centred * centred, axis=1, keepdims=True)
    normed = (centred * lax.rsqrt(spread + 1e-05) * gain).astype(BF16)
    packed = mm(normed, wqkv_ref[...])
    q_ref[rows] = packed[:, :C].astype(BF16)
    k_ref[rows] = (packed[:, C : 2 * C] * SCALE).astype(BF16)
    v_ref[rows] = packed[:, 2 * C :].astype(BF16)


def attend(q_ref, k_ref, v_ref, m_ref, line, tokens=slice(0, TOKENS)):
    group = 1 if line == 64 else 4
    for start in range(tokens.start, tokens.stop, line * group):
        rows = [slice(start + j * line, start + (j + 1) * line) for j in range(group)]
        some = [(q_ref[r], k_ref[r], v_ref[r]) for r in rows]
        mixed = [attend_64(*some[0])] if line == 64 else attend_128(some)
        for r, m in zip(rows, mixed):
            m_ref[r] = m.astype(BF16)


def reorder(source):
    r = lax.broadcasted_iota(jnp.int32, (BLOCK, BLOCK), 0)
    c = lax.broadcasted_iota(jnp.int32, (BLOCK, BLOCK), 1)
    return (c == source(r)).astype(F32).astype(BF16)


def chunk(i, size):
    return slice(i * size, (i + 1) * size)


def z_kernel(x_hbm, gain_hbm, wqkv_hbm, wo_hbm, o_ref, q_ref, k_ref, v_ref, m_ref, turn_ref, x_ref, gain_ref, wqkv_ref, wo_ref, sem):
    fetch = [
        pltpu.make_async_copy(gain_hbm, gain_ref, sem.at[0]),
        pltpu.make_async_copy(x_hbm.at[pl.ds(0, 1024)], x_ref.at[pl.ds(0, 1024)], sem.at[1]),
        pltpu.make_async_copy(wqkv_hbm.at[0], wqkv_ref, sem.at[2]),
        pltpu.make_async_copy(x_hbm.at[pl.ds(1024, 1024)], x_ref.at[pl.ds(1024, 1024)], sem.at[3]),
        pltpu.make_async_copy(wo_hbm.at[0], wo_ref, sem.at[4]),
    ]
    for copy in fetch:
        copy.start()
    turn_ref[...] = reorder(lambda r: r % 8 * 32 + r // 8)
    for i in range(2):
        for copy in (fetch[:3], fetch[3:])[i]:
            copy.wait()
        rows = slice(i * 1024, (i + 1) * 1024)
        project(x_ref[rows].astype(F32), gain_ref[0:1], wqkv_ref, q_ref, k_ref, v_ref, rows)

    attend(q_ref, k_ref, v_ref, m_ref, 64)

    for i in range(4):
        rows = chunk(i, 512)
        out = (x_ref[rows].astype(F32) + mm(m_ref[rows], wo_ref[...])).astype(BF16)
        for half in range(2):
            block = jnp.concatenate([out[y * 64 + half * 32 : y * 64 + half * 32 + 32] for y in range(8)], axis=0)
            turned = mm(turn_ref[...], block).astype(BF16)
            o_ref[half * 16 : half * 16 + 16, i] = turned.reshape(16, 16, C)


def y_kernel(x_ref, gain_ref, wqkv_ref, wo_ref, keep_ref, send_ref, q_ref, k_ref, v_ref, m_ref, turn_ref):
    me = lax.axis_index("core")

    def source(r):
        y_l = (r // 128 + me) % 2 * 4 + r // 8 % 4
        return r % 2 * 128 + r // 2 % 4 * 32 + r // 32 % 4 * 8 + y_l

    turn_ref[...] = reorder(source)

    def lines(zh, xl):
        s = x_ref[:, zh, xl].reshape(BLOCK, C).astype(F32)
        return jnp.concatenate([s[yb * 16 + zl * 8 : yb * 16 + zl * 8 + 8] for zl in range(2) for yb in range(16)], axis=0)

    for zh in range(2):
        s = jnp.concatenate([lines(zh, xl) for xl in range(4)], axis=0)
        project(s, gain_ref[1:2], wqkv_ref.at[1], q_ref, k_ref, v_ref, chunk(zh, 1024))

    attend(q_ref, k_ref, v_ref, m_ref, 128)

    for zh in range(2):
        update = mm(m_ref[chunk(zh, 1024)], wo_ref[1])
        for pair in range(2):
            turned = []
            for xl in (2 * pair, 2 * pair + 1):
                out = (lines(zh, xl) + update[xl * BLOCK : (xl + 1) * BLOCK]).astype(BF16)
                turned.append(mm(turn_ref[...], out))
            both = jnp.concatenate([t[g * 8 : g * 8 + 8] for g in range(32) for t in turned], axis=0).astype(BF16)
            keep_ref[:, :, 0, zh, pair] = both[:BLOCK].reshape(4, 4, 16, C)
            send_ref[:, :, zh, pair] = both[BLOCK:].reshape(4, 4, 16, C)


def x_kernel(x_ref, gain_ref, wqkv_ref, wo_ref, keep_ref, send_ref, q_ref, k_ref, v_ref, m_ref, turn_ref, s_ref):
    turn_ref[...] = reorder(lambda r: r % 32 // 2 * 16 + r % 2 * 8 + r // 32)

    for i in range(2):
        for j in range(2):
            for half in range(2):
                block = x_ref[i * 2 + j, half * 16 : half * 16 + 16].reshape(BLOCK, C)
                at = chunk(i * 2 + j, 8)
                s_ref[at, half * 32 : half * 32 + 32] = mm(turn_ref[...], block).astype(BF16).reshape(8, 32, C)
        s = s_ref[chunk(i, 16)].reshape(1024, C).astype(F32)
        project(s, gain_ref[2:3], wqkv_ref.at[2], q_ref, k_ref, v_ref, chunk(i, 1024))

    attend(q_ref, k_ref, v_ref, m_ref, 64)

    def source(r):
        return r // 8 % 2 * 128 + r % 2 * 64 + r // 32 % 4 * 16 + r // 128 * 8 + r // 16 % 2 * 4 + r // 2 % 4

    turn_ref[...] = reorder(source)

    for pair in range(2):
        s = s_ref[chunk(pair, 16)].reshape(1024, C).astype(F32)
        out = (s + mm(m_ref[chunk(pair, 1024)], wo_ref[2])).astype(BF16)
        for y_zl in range(4):
            block = jnp.concatenate([out[z * 512 + y_zl * 128 : z * 512 + y_zl * 128 + 128] for z in range(2)], axis=0)
            turned = mm(turn_ref[...], block).astype(BF16).reshape(2, 4, 2, 16, C)
            keep_ref[y_zl, :, :, 0, pair] = turned[0]
            send_ref[y_zl, :, :, pair] = turned[1]


def home_kernel(x_ref, o_ref):
    me = lax.axis_index("core")
    turn = reorder(lambda r: r // 16 % 4 * 64 + r // 2 % 2 * 32 + r // 4 % 4 * 8 + r // 64 * 2 + r % 2)
    for other in range(2):
        for y in range(4):
            block = x_ref[:, y, :, other].reshape(BLOCK, C)
            o_ref[:, (me + other) % 2 * 4 + y] = mm(turn, block).astype(BF16).reshape(4, 64, C)


WHOLE = pl.BlockSpec(memory_space=pltpu.VMEM)
HBM = pl.BlockSpec(memory_space=pltpu.HBM)


def axial_pass(kernel, x, gains, wqkv, wo, shapes, place=WHOLE, scratch=()):
    tokens = pltpu.VMEM((TOKENS, C), BF16)
    return pl.pallas_call(
        kernel,
        out_shape=[jax.ShapeDtypeStruct(shape, BF16) for shape in shapes],
        in_specs=[place] * 4,
        out_specs=[WHOLE] * len(shapes),
        scratch_shapes=[tokens] * 4 + [pltpu.VMEM((BLOCK, BLOCK), BF16), *scratch],
        compiler_params=pltpu.CompilerParams(vmem_limit_bytes=32 << 20),
    )(x, gains, wqkv, wo)


def z_pass(x, gains, wqkv, wo):
    fetched = [((TOKENS, C), BF16), ((3, C), F32), ((C, 3 * C), BF16), ((C, C), BF16)]
    scratch = [pltpu.VMEM(*f) for f in fetched] + [pltpu.SemaphoreType.DMA((5,))]
    fetch = [pltpu.with_memory_space_constraint(a, pltpu.HBM) for a in (x, gains, wqkv, wo)]
    return axial_pass(z_kernel, *fetch, [(32, 4, 16, C)], HBM, scratch)[0]


def y_pass(x, gains, wqkv, wo):
    return axial_pass(y_kernel, x, gains, wqkv, wo, [(4, 4, 2, 2, 2, 16, C), (4, 4, 2, 2, 16, C)])


def x_pass(x, gains, wqkv, wo):
    shapes = [(4, 4, 2, 2, 2, 16, C), (4, 4, 2, 2, 16, C)]
    return axial_pass(x_kernel, x, gains, wqkv, wo, shapes, scratch=[pltpu.VMEM((32, 64, C), BF16)])


def home(x):
    return pl.pallas_call(
        home_kernel,
        out_shape=jax.ShapeDtypeStruct((4, 8, 64, C), BF16),
        in_specs=[WHOLE],
        out_specs=WHOLE,
        compiler_params=pltpu.CompilerParams(vmem_limit_bytes=16 << 20),
    )(x)


def swap(keep, send, dests):
    got = lax.ppermute(send, "core", [(0, 1), (1, 0)])
    keep = keep.reshape(dests, 2, -1, C).at[:, 1].set(got.reshape(dests, -1, C))
    return keep.reshape(dests, -1, C)


def body(tokens, gains, wqkv, wo):
    weights = gains, wqkv, wo
    s = z_pass(tokens.reshape(TOKENS, C), *weights)
    s = lax.all_to_all(s.reshape(32, 64, C), ("zl", "x", "zh"), 0, 0, tiled=True)
    keep, send = y_pass(s.reshape(16, 2, 4, 16, C), *weights)
    s = lax.all_to_all(swap(keep, send, 16), ("x", "y"), 0, 0, tiled=True)
    keep, send = x_pass(s.reshape(4, 32, 16, C), *weights)
    s = lax.all_to_all(swap(keep, send, 32), ("zl", "y", "zh"), 0, 0, tiled=True)
    return home(s.reshape(4, 4, 2, 2, 32, C))


def solution(mesh):
    fine = Mesh(mesh.devices.reshape(4, 4, 4, 2, 2), ("zl", "x", "y", "zh", "core"))
    spec = P(("y", "zh", "core"), ("zl", "x"), None, None)
    return jax.shard_map(
        body, mesh=fine, in_specs=(spec, P(), P(), P()), out_specs=spec, check_vma=False
    )
```

```python
import functools

import jax
import jax.numpy as jnp
from jax import lax
from jax.experimental import pallas as pl
from jax.experimental.pallas import tpu as pltpu
from jax.sharding import Mesh, PartitionSpec as P

HEADS = 8
C = 256
HEAD = 32
UNIT = 128
BLOCK = 256
TOKENS = 2048
BF16 = jnp.bfloat16
F32 = jnp.float32
SCALE = HEAD ** (-0.5) * 1.4426950408889634
LOW = -1e30
NT = (((1,), (1,)), ((), ()))


def mm(a, b):
    return jnp.dot(a, b, preferred_element_type=F32)


def mm_nt(a, b):
    return lax.dot_general(a, b, NT, preferred_element_type=F32)


def lanes(n=C):
    return lax.broadcasted_iota(jnp.int32, (1, n), 1)


def two_halves(a):
    empty = jnp.zeros((a.shape[0], 128), BF16)
    return jnp.concatenate(
        [jnp.concatenate([a[:, :128], empty], axis=1), jnp.concatenate([empty, a[:, 128:]], axis=1)], axis=0
    )


def four_quarters(a):
    lane = lanes()
    zero = jnp.zeros((), BF16)
    return jnp.concatenate([jnp.where(lane // 64 == i, a, zero) for i in range(4)], axis=0)


def attend_64(q, k, v):
    lane = lanes()
    zero = jnp.zeros((), BF16)
    first = lane % 64 < HEAD
    own_q = jnp.concatenate([jnp.where(first, q, zero), jnp.where(first, zero, q)], axis=0)
    scores = mm_nt(own_q, four_quarters(k))
    left = lanes(128) < 64
    expo = []
    for half in range(2):
        s = scores[:, half * 128 : (half + 1) * 128]
        top_left = jnp.max(jnp.where(left, s, LOW), axis=1, keepdims=True)
        top_right = jnp.max(jnp.where(left, LOW, s), axis=1, keepdims=True)
        expo.append(jnp.exp2(s - jnp.where(left, top_left, top_right)).astype(BF16))
    expo = jnp.concatenate(expo, axis=1)
    mixed = mm(expo, four_quarters(v))
    total = mm(expo, four_quarters(jnp.ones((64, C), BF16)))
    return jnp.where(first, mixed[:64], mixed[64:]) / jnp.where(first, total[:64], total[64:])


def attend_128(q, k, v):
    slot = lanes() % 128 // HEAD
    zero = jnp.zeros((), BF16)
    own_q = jnp.concatenate([jnp.where(slot == j, q, zero) for j in range(4)], axis=0)
    scores = mm_nt(own_q, two_halves(k))

    def pick(a, slot):
        a = [a[j * UNIT : (j + 1) * UNIT] for j in range(4)]
        return jnp.where(slot == 0, a[0], jnp.where(slot == 1, a[1], jnp.where(slot == 2, a[2], a[3])))

    expos, totals = [], []
    for half in range(2):
        s = scores[:, half * 128 : (half + 1) * 128]
        expo = jnp.exp2(s - jnp.max(s, axis=1, keepdims=True))
        totals.append(pick(jnp.sum(expo, axis=1, keepdims=True), slot[:, :128]))
        expos.append(expo.astype(BF16))
    mixed = mm(jnp.concatenate(expos, axis=1), two_halves(v))
    return pick(mixed, slot) / jnp.concatenate(totals, axis=1)


def project(s, gain, wqkv_ref, q_ref, k_ref, v_ref, rows):
    centred = s - jnp.mean(s, axis=1, keepdims=True)
    spread = jnp.mean(centred * centred, axis=1, keepdims=True)
    normed = (centred * lax.rsqrt(spread + 1e-05) * gain).astype(BF16)
    packed = mm(normed, wqkv_ref[...])
    q_ref[rows] = packed[:, :C].astype(BF16)
    k_ref[rows] = (packed[:, C : 2 * C] * SCALE).astype(BF16)
    v_ref[rows] = packed[:, 2 * C :].astype(BF16)


def attend(q_ref, k_ref, v_ref, m_ref, line):
    one = attend_64 if line == 64 else attend_128
    for start in range(0, TOKENS, line):
        rows = slice(start, start + line)
        m_ref[rows] = one(q_ref[rows], k_ref[rows], v_ref[rows]).astype(BF16)


def reorder(source):
    r = lax.broadcasted_iota(jnp.int32, (BLOCK, BLOCK), 0)
    c = lax.broadcasted_iota(jnp.int32, (BLOCK, BLOCK), 1)
    return (c == source(r)).astype(F32).astype(BF16)


def chunk(i, size):
    return slice(i * size, (i + 1) * size)


def z_kernel(x_hbm, gain_hbm, wqkv_hbm, wo_hbm, o_ref, q_ref, k_ref, v_ref, m_ref, turn_ref, x_ref, gain_ref, wqkv_ref, wo_ref, sem):
    fetch = [
        pltpu.make_async_copy(gain_hbm, gain_ref, sem.at[0]),
        pltpu.make_async_copy(x_hbm.at[pl.ds(0, 1024)], x_ref.at[pl.ds(0, 1024)], sem.at[1]),
        pltpu.make_async_copy(wqkv_hbm.at[0], wqkv_ref, sem.at[2]),
        pltpu.make_async_copy(x_hbm.at[pl.ds(1024, 1024)], x_ref.at[pl.ds(1024, 1024)], sem.at[3]),
        pltpu.make_async_copy(wo_hbm.at[0], wo_ref, sem.at[4]),
    ]
    for copy in fetch:
        copy.start()
    turn_ref[...] = reorder(lambda r: r % 8 * 32 + r // 8)
    for i in range(2):
        for copy in (fetch[:3], fetch[3:])[i]:
            copy.wait()
        rows = slice(i * 1024, (i + 1) * 1024)
        project(x_ref[rows].astype(F32), gain_ref[0:1], wqkv_ref, q_ref, k_ref, v_ref, rows)

    attend(q_ref, k_ref, v_ref, m_ref, 64)

    for i in range(4):
        rows = chunk(i, 512)
        out = (x_ref[rows].astype(F32) + mm(m_ref[rows], wo_ref[...])).astype(BF16)
        for half in range(2):
            block = jnp.concatenate([out[y * 64 + half * 32 : y * 64 + half * 32 + 32] for y in range(8)], axis=0)
            turned = mm(turn_ref[...], block).astype(BF16)
            o_ref[half * 16 : half * 16 + 16, i] = turned.reshape(16, 16, C)


def y_kernel(x_ref, gain_ref, wqkv_ref, wo_ref, o_ref, q_ref, k_ref, v_ref, m_ref, turn_ref):
    def source(r):
        return r % 2 * 128 + r // 2 % 4 * 32 + r // 32 % 4 * 8 + r // 128 * 4 + r // 8 % 4

    turn_ref[...] = reorder(source)

    def lines(zh, xl):
        s = x_ref[:, zh, xl].reshape(BLOCK, C).astype(F32)
        return jnp.concatenate([s[yb * 16 + zl * 8 : yb * 16 + zl * 8 + 8] for zl in range(2) for yb in range(16)], axis=0)

    for zh in range(2):
        s = jnp.concatenate([lines(zh, xl) for xl in range(4)], axis=0)
        project(s, gain_ref[1:2], wqkv_ref.at[1], q_ref, k_ref, v_ref, chunk(zh, 1024))

    attend(q_ref, k_ref, v_ref, m_ref, 128)

    for zh in range(2):
        update = mm(m_ref[chunk(zh, 1024)], wo_ref[1])
        for pair in range(2):
            turned = []
            for xl in (2 * pair, 2 * pair + 1):
                out = (lines(zh, xl) + update[xl * BLOCK : (xl + 1) * BLOCK]).astype(BF16)
                turned.append(mm(turn_ref[...], out))
            both = jnp.concatenate([t[g * 8 : g * 8 + 8] for g in range(32) for t in turned], axis=0).astype(BF16)
            o_ref[:, :, :, zh, pair] = both.reshape(2, 4, 4, 16, C)


def x_kernel(x_ref, gain_ref, wqkv_ref, wo_ref, o_ref, q_ref, k_ref, v_ref, m_ref, turn_ref, s_ref):
    turn_ref[...] = reorder(lambda r: r % 32 // 2 * 16 + r % 2 * 8 + r // 32)

    for i in range(2):
        for z in (2 * i, 2 * i + 1):
            for c in range(2):
                block = x_ref[c, z].reshape(BLOCK, C)
                s_ref[chunk(z, 8), chunk(c, 32)] = mm(turn_ref[...], block).astype(BF16).reshape(8, 32, C)
        s = s_ref[chunk(i, 16)].reshape(1024, C).astype(F32)
        project(s, gain_ref[2:3], wqkv_ref.at[2], q_ref, k_ref, v_ref, chunk(i, 1024))

    attend(q_ref, k_ref, v_ref, m_ref, 64)

    def source(r):
        return r // 8 % 2 * 128 + r % 2 * 64 + r // 128 * 32 + r // 32 % 4 * 8 + r // 16 % 2 * 4 + r // 2 % 4

    turn_ref[...] = reorder(source)

    for pair in range(2):
        s = s_ref[chunk(pair, 16)].reshape(1024, C).astype(F32)
        out = (s + mm(m_ref[chunk(pair, 1024)], wo_ref[2])).astype(BF16)
        for y_zl in range(4):
            block = jnp.concatenate([out[z * 512 + y_zl * 128 : z * 512 + y_zl * 128 + 128] for z in range(2)], axis=0)
            o_ref[:, :, y_zl, :, pair] = mm(turn_ref[...], block).astype(BF16).reshape(2, 4, 2, 16, C)


def home_kernel(x_ref, o_hbm, out_ref, sem):
    turn = reorder(lambda r: r // 16 % 4 * 64 + r // 2 % 2 * 32 + r // 4 % 4 * 8 + r // 64 * 2 + r % 2)
    copies = []
    for y in range(8):
        out_ref[:, y] = mm(turn, x_ref[y].reshape(BLOCK, C)).astype(BF16).reshape(4, 64, C)
        if y % 2:
            some = pl.ds(y - 1, 2)
            copies.append(pltpu.make_async_copy(out_ref.at[:, some], o_hbm.at[:, some], sem.at[y // 2]))
            copies[-1].start()
    for copy in copies:
        copy.wait()


WHOLE = pl.BlockSpec(memory_space=pltpu.VMEM)
HBM = pl.BlockSpec(memory_space=pltpu.HBM)


def axial_pass(kernel, x, gains, wqkv, wo, shapes, place=WHOLE, scratch=()):
    tokens = pltpu.VMEM((TOKENS, C), BF16)
    return pl.pallas_call(
        kernel,
        out_shape=[jax.ShapeDtypeStruct(shape, BF16) for shape in shapes],
        in_specs=[place] * 4,
        out_specs=[WHOLE] * len(shapes),
        scratch_shapes=[tokens] * 4 + [pltpu.VMEM((BLOCK, BLOCK), BF16), *scratch],
        compiler_params=pltpu.CompilerParams(vmem_limit_bytes=32 << 20),
    )(x, gains, wqkv, wo)


def z_pass(x, gains, wqkv, wo):
    fetched = [((TOKENS, C), BF16), ((3, C), F32), ((C, 3 * C), BF16), ((C, C), BF16)]
    scratch = [pltpu.VMEM(*f) for f in fetched] + [pltpu.SemaphoreType.DMA((5,))]
    fetch = [pltpu.with_memory_space_constraint(a, pltpu.HBM) for a in (x, gains, wqkv, wo)]
    return axial_pass(z_kernel, *fetch, [(32, 4, 16, C)], HBM, scratch)[0]


def y_pass(x, gains, wqkv, wo):
    return axial_pass(y_kernel, x, gains, wqkv, wo, [(2, 4, 4, 2, 2, 16, C)])[0]


def x_pass(x, gains, wqkv, wo):
    return axial_pass(x_kernel, x, gains, wqkv, wo, [(2, 4, 4, 2, 2, 16, C)], scratch=[pltpu.VMEM((32, 64, C), BF16)])[0]


def home(x):
    return pl.pallas_call(
        home_kernel,
        out_shape=jax.ShapeDtypeStruct((4, 8, 64, C), BF16),
        in_specs=[WHOLE],
        out_specs=pl.BlockSpec(memory_space=pl.ANY),
        scratch_shapes=[pltpu.VMEM((4, 8, 64, C), BF16), pltpu.SemaphoreType.DMA((4,))],
        compiler_params=pltpu.CompilerParams(vmem_limit_bytes=16 << 20),
    )(x)


def move(x, axes, parts):
    return lax.all_to_all(x.reshape(parts, TOKENS // parts, C), axes, 0, 0, tiled=True)


def body(tokens, gains, wqkv, wo):
    weights = gains, wqkv, wo
    s = z_pass(tokens.reshape(TOKENS, C), *weights)
    s = move(s, ("zl", "x", "zh"), 32)
    s = y_pass(s.reshape(16, 2, 4, 16, C), *weights)
    s = move(s, ("core", "x", "y"), 32)
    s = x_pass(s.reshape(2, 4, 16, 16, C), *weights)
    s = move(s, ("core", "y", "zl", "zh"), 64)
    return home(s.reshape(8, 4, 2, 32, C))


def solution(mesh):
    fine = Mesh(mesh.devices.reshape(4, 4, 4, 2, 2), ("zl", "x", "y", "zh", "core"))
    spec = P(("y", "zh", "core"), ("zl", "x"), None, None)
    return jax.shard_map(
        body, mesh=fine, in_specs=(spec, P(), P(), P()), out_specs=spec, check_vma=False
    )
```

```python
import functools

import jax
import jax.numpy as jnp
from jax import lax
from jax.experimental import pallas as pl
from jax.experimental.pallas import tpu as pltpu
from jax.sharding import Mesh, PartitionSpec as P

HEADS = 8
C = 256
HEAD = 32
UNIT = 128
BLOCK = 256
TOKENS = 2048
BF16 = jnp.bfloat16
F32 = jnp.float32
SCALE = HEAD ** (-0.5) * 1.4426950408889634
LOW = -1e30
NT = (((1,), (1,)), ((), ()))


def mm(a, b):
    return jnp.dot(a, b, preferred_element_type=F32)


def mm_nt(a, b):
    return lax.dot_general(a, b, NT, preferred_element_type=F32)


def lanes(n=C):
    return lax.broadcasted_iota(jnp.int32, (1, n), 1)


def two_halves(a):
    empty = jnp.zeros((a.shape[0], 128), BF16)
    return jnp.concatenate(
        [jnp.concatenate([a[:, :128], empty], axis=1), jnp.concatenate([empty, a[:, 128:]], axis=1)], axis=0
    )


def four_quarters(a):
    lane = lanes()
    zero = jnp.zeros((), BF16)
    return jnp.concatenate([jnp.where(lane // 64 == i, a, zero) for i in range(4)], axis=0)


def attend_64(q, k, v):
    lane = lanes()
    zero = jnp.zeros((), BF16)
    first = lane % 64 < HEAD
    own_q = jnp.concatenate([jnp.where(first, q, zero), jnp.where(first, zero, q)], axis=0)
    scores = mm_nt(own_q, four_quarters(k))
    left = lanes(128) < 64
    expo = []
    for half in range(2):
        s = scores[:, half * 128 : (half + 1) * 128]
        top_left = jnp.max(jnp.where(left, s, LOW), axis=1, keepdims=True)
        top_right = jnp.max(jnp.where(left, LOW, s), axis=1, keepdims=True)
        expo.append(jnp.exp2(s - jnp.where(left, top_left, top_right)).astype(BF16))
    expo = jnp.concatenate(expo, axis=1)
    mixed = mm(expo, four_quarters(v))
    total = mm(expo, four_quarters(jnp.ones((64, C), BF16)))
    return jnp.where(first, mixed[:64], mixed[64:]) / jnp.where(first, total[:64], total[64:])


def attend_128(lines):
    slot = lanes() % 128 // HEAD
    zero = jnp.zeros((), BF16)
    expos = []
    for q, k, _ in lines:
        own_q = jnp.concatenate([jnp.where(slot == j, q, zero) for j in range(4)], axis=0)
        scores = mm_nt(own_q, two_halves(k))
        expo = []
        for half in range(2):
            s = scores[:, half * 128 : (half + 1) * 128]
            expo.append(jnp.exp2(s - jnp.max(s, axis=1, keepdims=True)).astype(BF16))
        expos.append(jnp.concatenate(expo, axis=1))

    def pick(a):
        a = [a[j * UNIT : (j + 1) * UNIT] for j in range(4)]
        return jnp.where(slot == 0, a[0], jnp.where(slot == 1, a[1], jnp.where(slot == 2, a[2], a[3])))

    totals = mm(jnp.concatenate(expos, axis=0), two_halves(jnp.ones((UNIT, C), BF16)))
    return [
        pick(mm(expo, two_halves(v))) / pick(totals[i * 4 * UNIT : (i + 1) * 4 * UNIT])
        for i, (expo, (_, _, v)) in enumerate(zip(expos, lines))
    ]


def project(s, gain, wqkv_ref, q_ref, k_ref, v_ref, rows):
    centred = s - jnp.mean(s, axis=1, keepdims=True)
    spread = jnp.mean(centred * centred, axis=1, keepdims=True)
    normed = (centred * lax.rsqrt(spread + 1e-05) * gain).astype(BF16)
    packed = mm(normed, wqkv_ref[...])
    q_ref[rows] = packed[:, :C].astype(BF16)
    k_ref[rows] = (packed[:, C : 2 * C] * SCALE).astype(BF16)
    v_ref[rows] = packed[:, 2 * C :].astype(BF16)


def attend(q_ref, k_ref, v_ref, m_ref, line, tokens=slice(0, TOKENS)):
    group = 1 if line == 64 else 4
    for start in range(tokens.start, tokens.stop, line * group):
        rows = [slice(start + j * line, start + (j + 1) * line) for j in range(group)]
        some = [(q_ref[r], k_ref[r], v_ref[r]) for r in rows]
        mixed = [attend_64(*some[0])] if line == 64 else attend_128(some)
        for r, m in zip(rows, mixed):
            m_ref[r] = m.astype(BF16)


def reorder(source):
    r = lax.broadcasted_iota(jnp.int32, (BLOCK, BLOCK), 0)
    c = lax.broadcasted_iota(jnp.int32, (BLOCK, BLOCK), 1)
    return (c == source(r)).astype(F32).astype(BF16)


def chunk(i, size):
    return slice(i * size, (i + 1) * size)


def z_kernel(x_hbm, gain_hbm, wqkv_hbm, wo_hbm, o_ref, q_ref, k_ref, v_ref, m_ref, turn_ref, x_ref, gain_ref, wqkv_ref, wo_ref, sem):
    fetch = [
        pltpu.make_async_copy(gain_hbm, gain_ref, sem.at[0]),
        pltpu.make_async_copy(x_hbm.at[pl.ds(0, 1024)], x_ref.at[pl.ds(0, 1024)], sem.at[1]),
        pltpu.make_async_copy(wqkv_hbm.at[0], wqkv_ref, sem.at[2]),
        pltpu.make_async_copy(x_hbm.at[pl.ds(1024, 1024)], x_ref.at[pl.ds(1024, 1024)], sem.at[3]),
        pltpu.make_async_copy(wo_hbm.at[0], wo_ref, sem.at[4]),
    ]
    for copy in fetch:
        copy.start()
    turn_ref[...] = reorder(lambda r: r % 8 * 32 + r // 128 * 16 + r // 16 % 2 * 8 + r // 32 % 4 * 2 + r // 8 % 2)
    for i in range(2):
        for copy in (fetch[:3], fetch[3:])[i]:
            copy.wait()
        rows = slice(i * 1024, (i + 1) * 1024)
        project(x_ref[rows].astype(F32), gain_ref[0:1], wqkv_ref, q_ref, k_ref, v_ref, rows)

    attend(q_ref, k_ref, v_ref, m_ref, 64)

    for i in range(4):
        rows = chunk(i, 512)
        out = (x_ref[rows].astype(F32) + mm(m_ref[rows], wo_ref[...])).astype(BF16)
        for half in range(2):
            block = jnp.concatenate([out[y * 64 + half * 32 : y * 64 + half * 32 + 32] for y in range(8)], axis=0)
            turned = mm(turn_ref[...], block).astype(BF16)
            o_ref[half * 16 : half * 16 + 16, i] = turned.reshape(16, 16, C)


def y_kernel(x_ref, gain_ref, wqkv_ref, wo_ref, o_ref, q_ref, k_ref, v_ref, m_ref, turn_ref):
    turn_ref[...] = reorder(lambda r: r % 8 * 32 + r // 32 % 4 * 8 + r // 128 * 4 + r // 8 % 4)

    def lines(zh, xl):
        s = x_ref[:, zh, xl].reshape(BLOCK, C).astype(F32)
        return jnp.concatenate([s[yb * 16 + zl * 8 : yb * 16 + zl * 8 + 8] for zl in range(2) for yb in range(16)], axis=0)

    def some_lines(zh):
        return jnp.concatenate([lines(zh, xl) for xl in range(4)], axis=0)

    for zh in range(2):
        project(some_lines(zh), gain_ref[1:2], wqkv_ref.at[1], q_ref, k_ref, v_ref, chunk(zh, 1024))

    attend(q_ref, k_ref, v_ref, m_ref, 128)

    for zh in range(2):
        rows = chunk(zh, 1024)
        k_ref[rows] = (some_lines(zh) + mm(m_ref[rows], wo_ref[1])).astype(BF16)
    for y_zl in range(4):
        turned = []
        for zl in range(2):
            starts = [x * BLOCK + zl * 128 + y_zl * 32 for x in range(8)]
            block = jnp.concatenate([k_ref[start : start + 32] for start in starts], axis=0)
            turned.append(mm(turn_ref[...], block))
        both = jnp.concatenate([t[chunk(g, 8)] for g in range(32) for t in turned], axis=0).astype(BF16)
        o_ref[:, :, :, y_zl] = both.reshape(2, 4, 4, 16, C)


def x_kernel(x_ref, gain_ref, wqkv_ref, wo_ref, o_ref, q_ref, k_ref, v_ref, m_ref, turn_ref):
    turn_ref[...] = reorder(lambda r: r % 8 * 32 + r // 8)

    def lines(z):
        s = x_ref[:, z].reshape(512, C).astype(F32)
        return jnp.concatenate([s[chunk(cy * 8 + line, 8)] for line in range(8) for cy in range(8)], axis=0)

    def some_lines(i):
        return jnp.concatenate([lines(2 * i), lines(2 * i + 1)], axis=0)

    for i in range(2):
        project(some_lines(i), gain_ref[2:3], wqkv_ref.at[2], q_ref, k_ref, v_ref, chunk(i, 1024))

    attend(q_ref, k_ref, v_ref, m_ref, 64)

    for i in range(2):
        rows = chunk(i, 1024)
        k_ref[rows] = (some_lines(i) + mm(m_ref[rows], wo_ref[2])).astype(BF16)
    for y_zl in range(4):
        for c in range(2):
            starts = [z * 512 + y_zl * 128 + zl * 64 + c * 32 for z in range(4) for zl in range(2)]
            block = jnp.concatenate([k_ref[start : start + 32] for start in starts], axis=0)
            o_ref[c, :, y_zl] = mm(turn_ref[...], block).astype(BF16).reshape(4, 2, 32, C)


def home_kernel(x_ref, o_hbm, out_ref, sem):
    copies = []
    for y in range(8):
        s = x_ref[y].reshape(BLOCK, C).astype(F32)
        out = jnp.concatenate([s[chunk(z * 4 + xl, 8)] for xl in range(4) for z in range(8)], axis=0)
        out_ref[:, y] = out.astype(BF16).reshape(4, 64, C)
        if y % 2:
            some = pl.ds(y - 1, 2)
            copies.append(pltpu.make_async_copy(out_ref.at[:, some], o_hbm.at[:, some], sem.at[y // 2]))
            copies[-1].start()
    for copy in copies:
        copy.wait()


WHOLE = pl.BlockSpec(memory_space=pltpu.VMEM)
HBM = pl.BlockSpec(memory_space=pltpu.HBM)


def axial_pass(kernel, x, gains, wqkv, wo, shapes, place=WHOLE, scratch=()):
    tokens = pltpu.VMEM((TOKENS, C), BF16)
    return pl.pallas_call(
        kernel,
        out_shape=[jax.ShapeDtypeStruct(shape, BF16) for shape in shapes],
        in_specs=[place] * 4,
        out_specs=[WHOLE] * len(shapes),
        scratch_shapes=[tokens] * 4 + [pltpu.VMEM((BLOCK, BLOCK), BF16), *scratch],
        compiler_params=pltpu.CompilerParams(vmem_limit_bytes=32 << 20),
    )(x, gains, wqkv, wo)


def z_pass(x, gains, wqkv, wo):
    fetched = [((TOKENS, C), BF16), ((3, C), F32), ((C, 3 * C), BF16), ((C, C), BF16)]
    scratch = [pltpu.VMEM(*f) for f in fetched] + [pltpu.SemaphoreType.DMA((5,))]
    fetch = [pltpu.with_memory_space_constraint(a, pltpu.HBM) for a in (x, gains, wqkv, wo)]
    return axial_pass(z_kernel, *fetch, [(32, 4, 16, C)], HBM, scratch)[0]


def y_pass(x, gains, wqkv, wo):
    return axial_pass(y_kernel, x, gains, wqkv, wo, [(2, 4, 4, 4, 16, C)])[0]


def x_pass(x, gains, wqkv, wo):
    return axial_pass(x_kernel, x, gains, wqkv, wo, [(2, 4, 4, 2, 32, C)])[0]


def home(x):
    return pl.pallas_call(
        home_kernel,
        out_shape=jax.ShapeDtypeStruct((4, 8, 64, C), BF16),
        in_specs=[WHOLE],
        out_specs=pl.BlockSpec(memory_space=pl.ANY),
        scratch_shapes=[pltpu.VMEM((4, 8, 64, C), BF16), pltpu.SemaphoreType.DMA((4,))],
        compiler_params=pltpu.CompilerParams(vmem_limit_bytes=16 << 20),
    )(x)


def move(x, axes, parts):
    return lax.all_to_all(x.reshape(parts, TOKENS // parts, C), axes, 0, 0, tiled=True)


def body(tokens, gains, wqkv, wo):
    weights = gains, wqkv, wo
    s = z_pass(tokens.reshape(TOKENS, C), *weights)
    s = move(s, ("zl", "x", "zh"), 32)
    s = y_pass(s.reshape(16, 2, 4, 16, C), *weights)
    s = move(s, ("core", "x", "y"), 32)
    s = x_pass(s.reshape(2, 4, 4, 4, 16, C), *weights)
    s = move(s, ("core", "y", "zl", "zh"), 64)
    return home(s.reshape(8, 8, 32, C))


def solution(mesh):
    fine = Mesh(mesh.devices.reshape(4, 4, 4, 2, 2), ("zl", "x", "y", "zh", "core"))
    spec = P(("y", "zh", "core"), ("zl", "x"), None, None)
    return jax.shard_map(
        body, mesh=fine, in_specs=(spec, P(), P(), P()), out_specs=spec, check_vma=False
    )
```

```python
import functools

import jax
import jax.numpy as jnp
from jax import lax
from jax.experimental import pallas as pl
from jax.experimental.pallas import tpu as pltpu
from jax.sharding import Mesh, PartitionSpec as P

HEADS = 8
C = 256
HEAD = 32
UNIT = 128
BLOCK = 256
TOKENS = 2048
BF16 = jnp.bfloat16
F32 = jnp.float32
SCALE = HEAD ** (-0.5) * 1.4426950408889634
LOW = -1e30
NT = (((1,), (1,)), ((), ()))


def mm(a, b):
    return jnp.dot(a, b, preferred_element_type=F32)


def mm_nt(a, b):
    return lax.dot_general(a, b, NT, preferred_element_type=F32)


def lanes(n=C):
    return lax.broadcasted_iota(jnp.int32, (1, n), 1)


def two_halves(a):
    empty = jnp.zeros((a.shape[0], 128), BF16)
    return jnp.concatenate(
        [jnp.concatenate([a[:, :128], empty], axis=1), jnp.concatenate([empty, a[:, 128:]], axis=1)], axis=0
    )


def four_quarters(a):
    lane = lanes()
    zero = jnp.zeros((), BF16)
    return jnp.concatenate([jnp.where(lane // 64 == i, a, zero) for i in range(4)], axis=0)


def attend_64(q, k, v):
    lane = lanes()
    zero = jnp.zeros((), BF16)
    first = lane % 64 < HEAD
    own_q = jnp.concatenate([jnp.where(first, q, zero), jnp.where(first, zero, q)], axis=0)
    scores = mm_nt(own_q, four_quarters(k))
    left = lanes(128) < 64
    expo = []
    for half in range(2):
        s = scores[:, half * 128 : (half + 1) * 128]
        top_left = jnp.max(jnp.where(left, s, LOW), axis=1, keepdims=True)
        top_right = jnp.max(jnp.where(left, LOW, s), axis=1, keepdims=True)
        expo.append(jnp.exp2(s - jnp.where(left, top_left, top_right)).astype(BF16))
    expo = jnp.concatenate(expo, axis=1)
    mixed = mm(expo, four_quarters(v))
    total = mm(expo, four_quarters(jnp.ones((64, C), BF16)))
    return jnp.where(first, mixed[:64], mixed[64:]) / jnp.where(first, total[:64], total[64:])


def attend_128(lines):
    slot = lanes() % 128 // HEAD
    zero = jnp.zeros((), BF16)
    expos = []
    for q, k, _ in lines:
        own_q = jnp.concatenate([jnp.where(slot == j, q, zero) for j in range(4)], axis=0)
        scores = mm_nt(own_q, two_halves(k))
        expo = []
        for half in range(2):
            s = scores[:, half * 128 : (half + 1) * 128]
            expo.append(jnp.exp2(s - jnp.max(s, axis=1, keepdims=True)).astype(BF16))
        expos.append(jnp.concatenate(expo, axis=1))

    def pick(a):
        a = [a[j * UNIT : (j + 1) * UNIT] for j in range(4)]
        return jnp.where(slot == 0, a[0], jnp.where(slot == 1, a[1], jnp.where(slot == 2, a[2], a[3])))

    totals = mm(jnp.concatenate(expos, axis=0), two_halves(jnp.ones((UNIT, C), BF16)))
    return [
        pick(mm(expo, two_halves(v))) / pick(totals[i * 4 * UNIT : (i + 1) * 4 * UNIT])
        for i, (expo, (_, _, v)) in enumerate(zip(expos, lines))
    ]


def project(s, gain, wqkv_ref, q_ref, k_ref, v_ref, rows):
    centred = s - jnp.mean(s, axis=1, keepdims=True)
    spread = jnp.mean(centred * centred, axis=1, keepdims=True)
    normed = (centred * lax.rsqrt(spread + 1e-05) * gain).astype(BF16)
    packed = mm(normed, wqkv_ref[...])
    q_ref[rows] = packed[:, :C].astype(BF16)
    k_ref[rows] = (packed[:, C : 2 * C] * SCALE).astype(BF16)
    v_ref[rows] = packed[:, 2 * C :].astype(BF16)


def attend(q_ref, k_ref, v_ref, m_ref, line, tokens=slice(0, TOKENS)):
    group = 1 if line == 64 else 4
    for start in range(tokens.start, tokens.stop, line * group):
        rows = [slice(start + j * line, start + (j + 1) * line) for j in range(group)]
        some = [(q_ref[r], k_ref[r], v_ref[r]) for r in rows]
        mixed = [attend_64(*some[0])] if line == 64 else attend_128(some)
        for r, m in zip(rows, mixed):
            m_ref[r] = m.astype(BF16)


def reorder(source):
    r = lax.broadcasted_iota(jnp.int32, (BLOCK, BLOCK), 0)
    c = lax.broadcasted_iota(jnp.int32, (BLOCK, BLOCK), 1)
    return (c == source(r)).astype(F32).astype(BF16)


def chunk(i, size):
    return slice(i * size, (i + 1) * size)


def z_kernel(x_hbm, gain_hbm, wqkv_hbm, wo_hbm, o_ref, q_ref, k_ref, v_ref, m_ref, turn_ref, x_ref, gain_ref, wqkv_ref, wo_ref, sem):
    fetch = [
        pltpu.make_async_copy(gain_hbm, gain_ref, sem.at[0]),
        pltpu.make_async_copy(x_hbm.at[pl.ds(0, 1024)], x_ref.at[pl.ds(0, 1024)], sem.at[1]),
        pltpu.make_async_copy(wqkv_hbm.at[0], wqkv_ref, sem.at[2]),
        pltpu.make_async_copy(x_hbm.at[pl.ds(1024, 1024)], x_ref.at[pl.ds(1024, 1024)], sem.at[3]),
        pltpu.make_async_copy(wo_hbm.at[0], wo_ref, sem.at[4]),
    ]
    for copy in fetch:
        copy.start()
    turn_ref[...] = reorder(lambda r: r % 8 * 32 + r // 32 % 2 * 16 + r // 16 % 2 * 8 + r // 64 * 2 + r // 8 % 2)
    for i in range(2):
        for copy in (fetch[:3], fetch[3:])[i]:
            copy.wait()
        rows = slice(i * 1024, (i + 1) * 1024)
        project(x_ref[rows].astype(F32), gain_ref[0:1], wqkv_ref, q_ref, k_ref, v_ref, rows)

    attend(q_ref, k_ref, v_ref, m_ref, 64)

    for i in range(4):
        rows = chunk(i, 512)
        out = (x_ref[rows].astype(F32) + mm(m_ref[rows], wo_ref[...])).astype(BF16)
        for half in range(2):
            block = jnp.concatenate([out[y * 64 + half * 32 : y * 64 + half * 32 + 32] for y in range(8)], axis=0)
            turned = mm(turn_ref[...], block).astype(BF16)
            o_ref[:, half * 2 : half * 2 + 2, :, i] = turned.reshape(4, 2, 2, 16, C)


def y_kernel(x_ref, gain_ref, wqkv_ref, wo_ref, o_ref, q_ref, k_ref, v_ref, m_ref, turn_ref):
    turn_ref[...] = reorder(lambda r: r % 8 * 32 + r // 32 % 4 * 8 + r // 128 * 4 + r // 8 % 4)

    def lines(zh, xl):
        s = x_ref[:, zh, xl].reshape(BLOCK, C).astype(F32)
        starts = [y_x * 64 + y_zl * 16 + zl * 8 for zl in range(2) for y_zl in range(4) for y_x in range(4)]
        return jnp.concatenate([s[start : start + 8] for start in starts], axis=0)

    def some_lines(zh):
        return jnp.concatenate([lines(zh, xl) for xl in range(4)], axis=0)

    for i in range(4):
        s = jnp.concatenate([lines(i // 2, i % 2 * 2), lines(i // 2, i % 2 * 2 + 1)], axis=0)
        project(s, gain_ref[1:2], wqkv_ref.at[1], q_ref, k_ref, v_ref, chunk(i, 512))

    attend(q_ref, k_ref, v_ref, m_ref, 128)

    for zh in range(2):
        rows = chunk(zh, 1024)
        k_ref[rows] = (some_lines(zh) + mm(m_ref[rows], wo_ref[1])).astype(BF16)
    for y_zl in range(4):
        turned = []
        for zl in range(2):
            starts = [x * BLOCK + zl * 128 + y_zl * 32 for x in range(8)]
            block = jnp.concatenate([k_ref[start : start + 32] for start in starts], axis=0)
            turned.append(mm(turn_ref[...], block))
        both = jnp.concatenate([t[chunk(g, 8)] for g in range(32) for t in turned], axis=0).astype(BF16)
        o_ref[:, :, :, y_zl] = both.reshape(2, 4, 4, 16, C)


def x_kernel(x_ref, gain_ref, wqkv_ref, wo_ref, o_ref, q_ref, k_ref, v_ref, m_ref, turn_ref):
    turn_ref[...] = reorder(lambda r: r % 8 * 32 + r // 8)

    def lines(z):
        s = x_ref[:, z].reshape(512, C).astype(F32)
        return jnp.concatenate([s[chunk(cy * 8 + line, 8)] for line in range(8) for cy in range(8)], axis=0)

    def some_lines(i):
        return jnp.concatenate([lines(2 * i), lines(2 * i + 1)], axis=0)

    for i in range(4):
        project(lines(i), gain_ref[2:3], wqkv_ref.at[2], q_ref, k_ref, v_ref, chunk(i, 512))

    attend(q_ref, k_ref, v_ref, m_ref, 64)

    for i in range(2):
        rows = chunk(i, 1024)
        k_ref[rows] = (some_lines(i) + mm(m_ref[rows], wo_ref[2])).astype(BF16)
    for y_zl in range(4):
        for c in range(2):
            starts = [z * 512 + y_zl * 128 + zl * 64 + c * 32 for z in range(4) for zl in range(2)]
            block = jnp.concatenate([k_ref[start : start + 32] for start in starts], axis=0)
            o_ref[c, :, y_zl] = mm(turn_ref[...], block).astype(BF16).reshape(4, 2, 32, C)


def home_kernel(x_ref, o_hbm, out_ref, sem):
    copies = []
    for y in range(8):
        s = x_ref[y].reshape(BLOCK, C).astype(F32)
        out = jnp.concatenate([s[chunk(z * 4 + xl, 8)] for xl in range(4) for z in range(8)], axis=0)
        out_ref[:, y] = out.astype(BF16).reshape(4, 64, C)
        if y % 2:
            some = pl.ds(y - 1, 2)
            copies.append(pltpu.make_async_copy(out_ref.at[:, some], o_hbm.at[:, some], sem.at[y // 2]))
            copies[-1].start()
    for copy in copies:
        copy.wait()


WHOLE = pl.BlockSpec(memory_space=pltpu.VMEM)
HBM = pl.BlockSpec(memory_space=pltpu.HBM)


def axial_pass(kernel, x, gains, wqkv, wo, shapes, place=WHOLE, scratch=()):
    tokens = pltpu.VMEM((TOKENS, C), BF16)
    return pl.pallas_call(
        kernel,
        out_shape=[jax.ShapeDtypeStruct(shape, BF16) for shape in shapes],
        in_specs=[place] * 4,
        out_specs=[WHOLE] * len(shapes),
        scratch_shapes=[tokens] * 4 + [pltpu.VMEM((BLOCK, BLOCK), BF16), *scratch],
        compiler_params=pltpu.CompilerParams(vmem_limit_bytes=32 << 20),
    )(x, gains, wqkv, wo)


def z_pass(x, gains, wqkv, wo):
    fetched = [((TOKENS, C), BF16), ((3, C), F32), ((C, 3 * C), BF16), ((C, C), BF16)]
    scratch = [pltpu.VMEM(*f) for f in fetched] + [pltpu.SemaphoreType.DMA((5,))]
    fetch = [pltpu.with_memory_space_constraint(a, pltpu.HBM) for a in (x, gains, wqkv, wo)]
    return axial_pass(z_kernel, *fetch, [(4, 4, 2, 4, 16, C)], HBM, scratch)[0]


def y_pass(x, gains, wqkv, wo):
    return axial_pass(y_kernel, x, gains, wqkv, wo, [(2, 4, 4, 4, 16, C)])[0]


def x_pass(x, gains, wqkv, wo):
    return axial_pass(x_kernel, x, gains, wqkv, wo, [(2, 4, 4, 2, 32, C)])[0]


def home(x):
    return pl.pallas_call(
        home_kernel,
        out_shape=jax.ShapeDtypeStruct((4, 8, 64, C), BF16),
        in_specs=[WHOLE],
        out_specs=pl.BlockSpec(memory_space=pl.ANY),
        scratch_shapes=[pltpu.VMEM((4, 8, 64, C), BF16), pltpu.SemaphoreType.DMA((4,))],
        compiler_params=pltpu.CompilerParams(vmem_limit_bytes=16 << 20),
    )(x)


def move(x, axes, parts):
    return lax.all_to_all(x.reshape(parts, TOKENS // parts, C), axes, 0, 0, tiled=True)


def body(tokens, gains, wqkv, wo):
    weights = gains, wqkv, wo
    s = z_pass(tokens.reshape(TOKENS, C), *weights)
    s = move(s, ("x", "zl", "zh"), 32)
    s = y_pass(s.reshape(16, 2, 4, 16, C), *weights)
    s = move(s, ("core", "x", "y"), 32)
    s = x_pass(s.reshape(2, 4, 4, 4, 16, C), *weights)
    s = move(s, ("core", "y", "zl", "zh"), 64)
    return home(s.reshape(8, 8, 32, C))


def solution(mesh):
    fine = Mesh(mesh.devices.reshape(4, 4, 4, 2, 2), ("zl", "x", "y", "zh", "core"))
    spec = P(("y", "zh", "core"), ("zl", "x"), None, None)
    return jax.shard_map(
        body, mesh=fine, in_specs=(spec, P(), P(), P()), out_specs=spec, check_vma=False
    )
```

```python
import functools

import jax
import jax.numpy as jnp
from jax import lax
from jax.experimental import pallas as pl
from jax.experimental.pallas import tpu as pltpu
from jax.sharding import Mesh, PartitionSpec as P

HEADS = 8
C = 256
HEAD = 32
UNIT = 128
BLOCK = 256
TOKENS = 2048
BF16 = jnp.bfloat16
F32 = jnp.float32
SCALE = HEAD ** (-0.5) * 1.4426950408889634
LOW = -1e30
NT = (((1,), (1,)), ((), ()))


def mm(a, b):
    return jnp.dot(a, b, preferred_element_type=F32)


def mm_nt(a, b):
    return lax.dot_general(a, b, NT, preferred_element_type=F32)


def lanes(n=C):
    return lax.broadcasted_iota(jnp.int32, (1, n), 1)


def two_halves(a):
    empty = jnp.zeros((a.shape[0], 128), BF16)
    return jnp.concatenate(
        [jnp.concatenate([a[:, :128], empty], axis=1), jnp.concatenate([empty, a[:, 128:]], axis=1)], axis=0
    )


def four_quarters(a):
    lane = lanes()
    zero = jnp.zeros((), BF16)
    return jnp.concatenate([jnp.where(lane // 64 == i, a, zero) for i in range(4)], axis=0)


def attend_64(q, k, v):
    lane = lanes()
    zero = jnp.zeros((), BF16)
    first = lane % 64 < HEAD
    own_q = jnp.concatenate([jnp.where(first, q, zero), jnp.where(first, zero, q)], axis=0)
    scores = mm_nt(own_q, four_quarters(k))
    left = lanes(128) < 64
    expo = []
    for half in range(2):
        s = scores[:, half * 128 : (half + 1) * 128]
        top_left = jnp.max(jnp.where(left, s, LOW), axis=1, keepdims=True)
        top_right = jnp.max(jnp.where(left, LOW, s), axis=1, keepdims=True)
        expo.append(jnp.exp2(s - jnp.where(left, top_left, top_right)).astype(BF16))
    expo = jnp.concatenate(expo, axis=1)
    mixed = mm(expo, four_quarters(v))
    total = mm(expo, four_quarters(jnp.ones((64, C), BF16)))
    return jnp.where(first, mixed[:64], mixed[64:]) / jnp.where(first, total[:64], total[64:])


def attend_128(lines):
    slot = lanes() % 128 // HEAD
    zero = jnp.zeros((), BF16)
    expos = []
    for q, k, _ in lines:
        own_q = jnp.concatenate([jnp.where(slot == j, q, zero) for j in range(4)], axis=0)
        scores = mm_nt(own_q, two_halves(k))
        expo = []
        for half in range(2):
            s = scores[:, half * 128 : (half + 1) * 128]
            expo.append(jnp.exp2(s - jnp.max(s, axis=1, keepdims=True)).astype(BF16))
        expos.append(jnp.concatenate(expo, axis=1))

    def pick(a):
        a = [a[j * UNIT : (j + 1) * UNIT] for j in range(4)]
        return jnp.where(slot == 0, a[0], jnp.where(slot == 1, a[1], jnp.where(slot == 2, a[2], a[3])))

    totals = mm(jnp.concatenate(expos, axis=0), two_halves(jnp.ones((UNIT, C), BF16)))
    return [
        pick(mm(expo, two_halves(v))) / pick(totals[i * 4 * UNIT : (i + 1) * 4 * UNIT])
        for i, (expo, (_, _, v)) in enumerate(zip(expos, lines))
    ]


def project(s, gain, wqkv_ref, q_ref, k_ref, v_ref, rows):
    centred = s - jnp.mean(s, axis=1, keepdims=True)
    spread = jnp.mean(centred * centred, axis=1, keepdims=True)
    normed = (centred * lax.rsqrt(spread + 1e-05) * gain).astype(BF16)
    packed = mm(normed, wqkv_ref[...])
    q_ref[rows] = packed[:, :C].astype(BF16)
    k_ref[rows] = (packed[:, C : 2 * C] * SCALE).astype(BF16)
    v_ref[rows] = packed[:, 2 * C :].astype(BF16)


def attend(q_ref, k_ref, v_ref, m_ref, line, tokens=slice(0, TOKENS)):
    group = 1 if line == 64 else 4
    for start in range(tokens.start, tokens.stop, line * group):
        rows = [slice(start + j * line, start + (j + 1) * line) for j in range(group)]
        some = [(q_ref[r], k_ref[r], v_ref[r]) for r in rows]
        mixed = [attend_64(*some[0])] if line == 64 else attend_128(some)
        for r, m in zip(rows, mixed):
            m_ref[r] = m.astype(BF16)


def reorder(source):
    r = lax.broadcasted_iota(jnp.int32, (BLOCK, BLOCK), 0)
    c = lax.broadcasted_iota(jnp.int32, (BLOCK, BLOCK), 1)
    return (c == source(r)).astype(F32).astype(BF16)


def chunk(i, size):
    return slice(i * size, (i + 1) * size)


def z_kernel(x_hbm, gain_hbm, wqkv_hbm, wo_hbm, o_ref, q_ref, k_ref, v_ref, m_ref, turn_ref, x_ref, gain_ref, wqkv_ref, wo_ref, sem):
    fetch = [
        pltpu.make_async_copy(gain_hbm, gain_ref, sem.at[0]),
        pltpu.make_async_copy(x_hbm.at[pl.ds(0, 1024)], x_ref.at[pl.ds(0, 1024)], sem.at[1]),
        pltpu.make_async_copy(wqkv_hbm.at[0], wqkv_ref, sem.at[2]),
        pltpu.make_async_copy(x_hbm.at[pl.ds(1024, 1024)], x_ref.at[pl.ds(1024, 1024)], sem.at[3]),
        pltpu.make_async_copy(wo_hbm.at[0], wo_ref, sem.at[4]),
    ]
    for copy in fetch:
        copy.start()
    turn_ref[...] = reorder(lambda r: r % 8 * 32 + r // 32 % 2 * 16 + r // 16 % 2 * 8 + r // 64 * 2 + r // 8 % 2)
    for i in range(2):
        for copy in (fetch[:3], fetch[3:])[i]:
            copy.wait()
        rows = slice(i * 1024, (i + 1) * 1024)
        project(x_ref[rows].astype(F32), gain_ref[0:1], wqkv_ref, q_ref, k_ref, v_ref, rows)

    attend(q_ref, k_ref, v_ref, m_ref, 64)

    for i in range(4):
        rows = chunk(i, 512)
        out = (x_ref[rows].astype(F32) + mm(m_ref[rows], wo_ref[...])).astype(BF16)
        for half in range(2):
            block = jnp.concatenate([out[y * 64 + half * 32 : y * 64 + half * 32 + 32] for y in range(8)], axis=0)
            turned = mm(turn_ref[...], block).astype(BF16)
            o_ref[:, half * 2 : half * 2 + 2, :, i] = turned.reshape(4, 2, 2, 16, C)


def y_kernel(x_ref, gain_ref, wqkv_ref, wo_ref, o_ref, q_ref, k_ref, v_ref, m_ref, turn_ref):
    turn_ref[...] = reorder(lambda r: r % 8 * 32 + r // 32 % 4 * 8 + r // 128 * 4 + r // 8 % 4)

    def lines(zh, xl):
        s = x_ref[:, zh, xl].reshape(BLOCK, C).astype(F32)
        starts = [y_x * 64 + y_zl * 16 + zl * 8 for zl in range(2) for y_zl in range(4) for y_x in range(4)]
        return jnp.concatenate([s[start : start + 8] for start in starts], axis=0)

    def some_lines(zh):
        return jnp.concatenate([lines(zh, xl) for xl in range(4)], axis=0)

    for i in range(4):
        s = jnp.concatenate([lines(i // 2, i % 2 * 2), lines(i // 2, i % 2 * 2 + 1)], axis=0)
        project(s, gain_ref[1:2], wqkv_ref.at[1], q_ref, k_ref, v_ref, chunk(i, 512))

    attend(q_ref, k_ref, v_ref, m_ref, 128)

    for zh in range(2):
        rows = chunk(zh, 1024)
        k_ref[rows] = (some_lines(zh) + mm(m_ref[rows], wo_ref[1])).astype(BF16)
    for y_zl in range(4):
        turned = []
        for zl in range(2):
            starts = [x * BLOCK + zl * 128 + y_zl * 32 for x in range(8)]
            block = jnp.concatenate([k_ref[start : start + 32] for start in starts], axis=0)
            turned.append(mm(turn_ref[...], block))
        both = jnp.concatenate([t[chunk(g, 8)] for g in range(32) for t in turned], axis=0).astype(BF16)
        o_ref[:, :, :, y_zl] = both.reshape(2, 4, 4, 16, C)


def x_kernel(x_ref, gain_ref, wqkv_ref, wo_ref, o_ref, q_ref, k_ref, v_ref, m_ref, turn_ref):
    turn_ref[...] = reorder(lambda r: r % 8 * 32 + r // 8)

    def lines(z):
        s = x_ref[:, z].reshape(512, C).astype(F32)
        return jnp.concatenate([s[chunk(cy * 8 + line, 8)] for line in range(8) for cy in range(8)], axis=0)

    def some_lines(i):
        return jnp.concatenate([lines(2 * i), lines(2 * i + 1)], axis=0)

    for i in range(4):
        project(lines(i), gain_ref[2:3], wqkv_ref.at[2], q_ref, k_ref, v_ref, chunk(i, 512))

    attend(q_ref, k_ref, v_ref, m_ref, 64)

    for i in range(2):
        rows = chunk(i, 1024)
        k_ref[rows] = (some_lines(i) + mm(m_ref[rows], wo_ref[2])).astype(BF16)
    for y_zl in range(4):
        for c in range(2):
            starts = [z * 512 + y_zl * 128 + zl * 64 + c * 32 for z in range(4) for zl in range(2)]
            block = jnp.concatenate([k_ref[start : start + 32] for start in starts], axis=0)
            o_ref[c, :, y_zl] = mm(turn_ref[...], block).astype(BF16).reshape(4, 2, 32, C)


def home_kernel(x_ref, o_hbm, out_ref, sem):
    copies = []
    for y in range(8):
        s = x_ref[y].reshape(BLOCK, C).astype(F32)
        out = jnp.concatenate([s[chunk(z * 4 + xl, 8)] for xl in range(4) for z in range(8)], axis=0)
        out_ref[:, y] = out.astype(BF16).reshape(4, 64, C)
        copies.append(pltpu.make_async_copy(out_ref.at[:, y], o_hbm.at[:, y], sem.at[y]))
        copies[-1].start()
    for copy in copies:
        copy.wait()


WHOLE = pl.BlockSpec(memory_space=pltpu.VMEM)
HBM = pl.BlockSpec(memory_space=pltpu.HBM)


def axial_pass(kernel, x, gains, wqkv, wo, shapes, place=WHOLE, scratch=()):
    tokens = pltpu.VMEM((TOKENS, C), BF16)
    return pl.pallas_call(
        kernel,
        out_shape=[jax.ShapeDtypeStruct(shape, BF16) for shape in shapes],
        in_specs=[place] * 4,
        out_specs=[WHOLE] * len(shapes),
        scratch_shapes=[tokens] * 4 + [pltpu.VMEM((BLOCK, BLOCK), BF16), *scratch],
        compiler_params=pltpu.CompilerParams(vmem_limit_bytes=32 << 20),
    )(x, gains, wqkv, wo)


def z_pass(x, gains, wqkv, wo):
    fetched = [((TOKENS, C), BF16), ((3, C), F32), ((C, 3 * C), BF16), ((C, C), BF16)]
    scratch = [pltpu.VMEM(*f) for f in fetched] + [pltpu.SemaphoreType.DMA((5,))]
    fetch = [pltpu.with_memory_space_constraint(a, pltpu.HBM) for a in (x, gains, wqkv, wo)]
    return axial_pass(z_kernel, *fetch, [(4, 4, 2, 4, 16, C)], HBM, scratch)[0]


def y_pass(x, gains, wqkv, wo):
    return axial_pass(y_kernel, x, gains, wqkv, wo, [(2, 4, 4, 4, 16, C)])[0]


def x_pass(x, gains, wqkv, wo):
    return axial_pass(x_kernel, x, gains, wqkv, wo, [(2, 4, 4, 2, 32, C)])[0]


def home(x):
    return pl.pallas_call(
        home_kernel,
        out_shape=jax.ShapeDtypeStruct((4, 8, 64, C), BF16),
        in_specs=[WHOLE],
        out_specs=pl.BlockSpec(memory_space=pl.ANY),
        scratch_shapes=[pltpu.VMEM((4, 8, 64, C), BF16), pltpu.SemaphoreType.DMA((8,))],
        compiler_params=pltpu.CompilerParams(vmem_limit_bytes=16 << 20),
    )(x)


def move(x, axes, parts):
    return lax.all_to_all(x.reshape(parts, TOKENS // parts, C), axes, 0, 0, tiled=True)


def body(tokens, gains, wqkv, wo):
    weights = gains, wqkv, wo
    s = z_pass(tokens.reshape(TOKENS, C), *weights)
    s = move(s, ("x", "zl", "zh"), 32)
    s = y_pass(s.reshape(16, 2, 4, 16, C), *weights)
    s = move(s, ("core", "x", "y"), 32)
    s = x_pass(s.reshape(2, 4, 4, 4, 16, C), *weights)
    s = move(s, ("core", "y", "zl", "zh"), 64)
    return home(s.reshape(8, 8, 32, C))


def solution(mesh):
    fine = Mesh(mesh.devices.reshape(4, 4, 4, 2, 2), ("zl", "x", "y", "zh", "core"))
    spec = P(("y", "zh", "core"), ("zl", "x"), None, None)
    return jax.shard_map(
        body, mesh=fine, in_specs=(spec, P(), P(), P()), out_specs=spec, check_vma=False
    )
```
